32 devices in a mesh: dp: 4 (over z), space: 8 (over y, x, core).
Axes of the slice: x: 2, y: 2, z: 4, core: 2. Of those that a mesh axis runs over, the one named last changes fastest.
Arguments:
- features: bfloat16 [4, 32, 32, 32, 128], P('dp', None, 'space'), may hold values from -6 to 6
- cotangent: bfloat16 [4, 32, 32, 32, 128], P('dp', None, 'space'), may hold values from -6 to 6
- spectral: bfloat16 [256, 32, 2048], P('space', 'dp'), may hold values from -1.5 to 1.5
- pointwise: bfloat16 [32, 32], replicated, may hold values from -1 to 1
- biases: bfloat16 [32], replicated, may hold values from -3 to 3
Outputs:
- grad_input: bfloat16 [4, 32, 32, 32, 128], P('dp', None, 'space')
- grad_spectral: float32 [256, 32, 2048], P('space', 'dp')
The draws below stay inside these ranges and needn't reach their ends.
All inputs are finite; a program needn't handle non-finite values.
Results may differ from the reference program's by a relative error of at most 0.025.
Values may be sent and summed in bfloat16 or wider, within the bound.
A program may use at most 128 MiB of HBM per device.

```python
import math
import jax
import jax.numpy as jnp
from jax import lax

C = 32
KX = 32
KY = 32
KZ = 8
NY = 32
NZ = 128
NX = 32
SAMPLES = 4


def levels(rng, dims, cuts, least, high):
    gain, own = 1.0, jax.random.fold_in(rng, 6)
    for axis_at, parts in cuts:
        heights = jnp.exp(jax.random.uniform(jax.random.fold_in(own, axis_at), (parts,), jnp.float32, least / len(cuts), high / len(cuts)))
        gain = gain * jnp.repeat(heights, dims[axis_at] // parts).reshape([-1 if axis == axis_at else 1 for axis in range(len(dims))])
    return gain


def noise(own_key, dims, spread, most, pieces=(), kind=jnp.bfloat16):
    gain = levels(own_key, dims, pieces, -0.22, 0.18) if pieces else 1.0
    array = jax.random.normal(own_key, dims, jnp.float32) * spread * gain
    return jnp.minimum(jnp.maximum(array, -most), most).astype(kind)


def setup_inputs(seed: int = 0) -> dict:
    keys = jax.random.split(jax.random.key(seed), 6)
    return {
        "features": noise(keys[0], (SAMPLES, C, NX, NY, NZ), 1.0, 6.0, ((0, 4), (2, 8))),
        "cotangent": noise(keys[1], (SAMPLES, C, NX, NY, NZ), 1.0, 6.0, ((0, 4), (2, 8))),
        "spectral": noise(keys[2], (KY * KZ, KX, 2 * C * C), (max(1, 8 * KX * KY * KZ * C // (NX * NY * NZ))) ** -0.5, 1.5, ((0, 8), (1, 4))),
        "pointwise": noise(keys[3], (C, C), C ** -0.5, 1.0),
        "biases": noise(keys[4], (C,), 0.5, 3.0),
    }


tanh_coef = 0.7978845608028654
cubic_coef = 0.044715

def frequencies(kept_count, length):
    indices = jnp.arange(kept_count, dtype=jnp.int32)
    return jnp.where(indices < kept_count // 2, indices, indices + (length - kept_count))

def plane_table(count_y, count_z, kept_y, kept_z):
    freq_y = frequencies(kept_y, count_y)
    freq_z = jnp.arange(kept_z, dtype=jnp.int32)
    turn_y = jnp.arange(count_y, dtype=jnp.int32)[:, None] * freq_y[None, :] % count_y
    turn_z = jnp.arange(count_z, dtype=jnp.int32)[:, None] * freq_z[None, :] % count_z
    angles = 2.0 * math.pi * (turn_y[:, None, :, None].astype(jnp.float32) / count_y + turn_z[None, :, None, :].astype(jnp.float32) / count_z)
    factor = 1.0 / math.sqrt(count_y * count_z)
    basis_table = jnp.stack([factor * jnp.cos(angles), -factor * jnp.sin(angles)], axis=-1)
    return basis_table.reshape(count_y * count_z, kept_y * kept_z, 2).astype(jnp.bfloat16)

def line_table(full_length, kept_count):
    freq_x = frequencies(kept_count, full_length)
    turns = jnp.arange(full_length, dtype=jnp.int32)[:, None] * freq_x[None, :] % full_length
    angles = 2.0 * math.pi * turns.astype(jnp.float32) / full_length
    factor = 1.0 / math.sqrt(full_length)
    cos_part = factor * jnp.cos(angles)
    sine_part = factor * jnp.sin(angles)
    first_row = jnp.stack([cos_part, -sine_part], axis=1)
    second = jnp.stack([sine_part, cos_part], axis=1)
    return jnp.stack([first_row, second], axis=0).astype(jnp.bfloat16)

def mode_doubling(kept_y, kept_z):
    mode_index = jnp.arange(kept_y * kept_z, dtype=jnp.int32) % kept_z
    return jnp.where(mode_index == 0, 1.0, 2.0).astype(jnp.float32)

def gelu_slope(values):
    inner_arg = tanh_coef * (values + cubic_coef * values * values * values)
    tanh_part = jnp.tanh(inner_arg)
    return 0.5 * (1.0 + tanh_part) + 0.5 * values * (1.0 - tanh_part * tanh_part) * tanh_coef * (1.0 + 3.0 * cubic_coef * values * values)

def product(equation, left_op, right_op):
    return jnp.einsum(equation, left_op.astype(jnp.float32), right_op.astype(jnp.float32))

def forward_lines(coarse, line_basis):
    return product('xpscm,pxqk->kqscm', coarse, line_basis).astype(jnp.bfloat16)

def inverse_lines(spectrum, line_basis):
    return product('kqscm,pxqk->xpscm', spectrum, line_basis).astype(jnp.bfloat16)

def spectral_mix(spectrum, weights):
    real_part = spectrum[:, 0]
    imag_part = spectrum[:, 1]
    w_real = weights[:, :, 0]
    w_imag = weights[:, :, 1]
    out_real = product('ksim,mkio->ksom', real_part, w_real) - product('ksim,mkio->ksom', imag_part, w_imag)
    out_imag = product('ksim,mkio->ksom', real_part, w_imag) + product('ksim,mkio->ksom', imag_part, w_real)
    return jnp.stack([out_real, out_imag], axis=1).astype(jnp.bfloat16)

def spectral_pull(adjoint, weights):
    real_part = adjoint[:, 0]
    imag_part = adjoint[:, 1]
    w_real = weights[:, :, 0]
    w_imag = weights[:, :, 1]
    out_real = product('ksom,mkio->ksim', real_part, w_real) + product('ksom,mkio->ksim', imag_part, w_imag)
    out_imag = product('ksom,mkio->ksim', imag_part, w_real) - product('ksom,mkio->ksim', real_part, w_imag)
    return jnp.stack([out_real, out_imag], axis=1).astype(jnp.bfloat16)

def weight_grad(spectrum, adjoint):
    spec_real = spectrum[:, 0]
    spec_imag = spectrum[:, 1]
    adj_real = adjoint[:, 0]
    adj_imag = adjoint[:, 1]
    grad_real = product('ksim,ksom->mkio', spec_real, adj_real) + product('ksim,ksom->mkio', spec_imag, adj_imag)
    grad_imag = product('ksim,ksom->mkio', spec_real, adj_imag) - product('ksim,ksom->mkio', spec_imag, adj_real)
    return jnp.stack([grad_real, grad_imag], axis=2)

def reference(features, cotangent, spectral, pointwise, biases):
    full_length = features.shape[2]
    plane_basis = plane_table(NY, NZ, KY, KZ)
    line_basis = line_table(full_length, KX)
    doubling = mode_doubling(KY, KZ)
    weights = spectral.reshape(KY * KZ, KX, 2, C, C)

    def one_sample(running, sample_pair):
        sample_in, sample_grad = sample_pair
        flat_cells = sample_in.reshape(1, C, full_length, NY * NZ)
        coarse = product('scxq,qmp->xpscm', flat_cells, plane_basis).astype(jnp.bfloat16)
        spectrum = forward_lines(coarse, line_basis)
        mixed_modes = spectral_mix(spectrum, weights)
        returned = inverse_lines(mixed_modes, line_basis)
        scaled = returned.astype(jnp.float32) * doubling[None, None, None, None, :]
        spectral_part = product('xpscm,qmp->scxq', scaled, plane_basis)
        linear = product('sicq,io->socq', flat_cells, pointwise)
        pre_act = linear + biases.astype(jnp.float32)[None, :, None, None] + spectral_part
        upstream_grad = sample_grad.reshape(1, C, full_length, NY * NZ).astype(jnp.float32)
        delta_cells = (upstream_grad * gelu_slope(pre_act)).astype(jnp.bfloat16)
        coarse_back = (product('scxq,qmp->xpscm', delta_cells, plane_basis) * doubling[None, None, None, None, :]).astype(jnp.bfloat16)
        adjoint = forward_lines(coarse_back, line_basis)
        pulled = spectral_pull(adjoint, weights)
        grad_terms = weight_grad(spectrum, adjoint)
        back_cells = inverse_lines(pulled, line_basis)
        grad_cells = product('socq,io->sicq', delta_cells, pointwise) + product('xpscm,qmp->scxq', back_cells, plane_basis)
        return (running + grad_terms, grad_cells.astype(jnp.bfloat16).reshape(C, full_length, NY, NZ))
    start_sum = jnp.zeros((KY * KZ, KX, 2, C, C), jnp.float32)
    running, grad_input = lax.scan(one_sample, start_sum, (features, cotangent))
    return (grad_input, running.reshape(KY * KZ, KX, 2 * C * C))
```

```python
import functools
import math

import jax
import jax.numpy as jnp
import ml_dtypes
import numpy as np
from jax import lax
from jax.experimental import pallas as pl
from jax.experimental.pallas import tpu as pltpu
from jax.sharding import PartitionSpec as P

KX = 32
KY = 32
KZ = 8


tanh_coef = 0.7978845608028654
cubic_coef = 0.044715


def frequencies(kept_count, length):
    indices = jnp.arange(kept_count, dtype=jnp.int32)
    return jnp.where(indices < kept_count // 2, indices, indices + (length - kept_count))


def plane_table(count_y, count_z, kept_y, kept_z):
    freq_y = frequencies(kept_y, count_y)
    freq_z = jnp.arange(kept_z, dtype=jnp.int32)
    turn_y = jnp.arange(count_y, dtype=jnp.int32)[:, None] * freq_y[None, :] % count_y
    turn_z = jnp.arange(count_z, dtype=jnp.int32)[:, None] * freq_z[None, :] % count_z
    angles = (
        2.0
        * math.pi
        * (
            turn_y[:, None, :, None].astype(jnp.float32) / count_y
            + turn_z[None, :, None, :].astype(jnp.float32) / count_z
        )
    )
    factor = 1.0 / math.sqrt(count_y * count_z)
    basis_table = jnp.stack([factor * jnp.cos(angles), -factor * jnp.sin(angles)], axis=-1)
    return basis_table.reshape(count_y * count_z, kept_y * kept_z, 2).astype(jnp.bfloat16)


def line_table(full_length, kept_count):
    freq_x = frequencies(kept_count, full_length)
    turns = jnp.arange(full_length, dtype=jnp.int32)[:, None] * freq_x[None, :] % full_length
    angles = 2.0 * math.pi * turns.astype(jnp.float32) / full_length
    factor = 1.0 / math.sqrt(full_length)
    cos_part = factor * jnp.cos(angles)
    sine_part = factor * jnp.sin(angles)
    first_row = jnp.stack([cos_part, -sine_part], axis=1)
    second = jnp.stack([sine_part, cos_part], axis=1)
    return jnp.stack([first_row, second], axis=0).astype(jnp.bfloat16)


def mode_doubling(kept_y, kept_z):
    mode_index = jnp.arange(kept_y * kept_z, dtype=jnp.int32) % kept_z
    return jnp.where(mode_index == 0, 1.0, 2.0).astype(jnp.float32)


def gelu_slope(values):
    inner_arg = tanh_coef * (values + cubic_coef * values * values * values)
    tanh_part = jnp.tanh(inner_arg)
    return 0.5 * (1.0 + tanh_part) + 0.5 * values * (1.0 - tanh_part * tanh_part) * tanh_coef * (
        1.0 + 3.0 * cubic_coef * values * values
    )


def product(equation, left_op, right_op):
    return jnp.einsum(equation, left_op, right_op, preferred_element_type=jnp.float32)


def forward_lines(coarse, line_basis):
    return product("xpscm,pxqk->kqscm", coarse, line_basis).astype(jnp.bfloat16)


def inverse_lines(spectrum, line_basis):
    return product("kqscm,pxqk->xpscm", spectrum, line_basis).astype(jnp.bfloat16)


def spectral_mix(spectrum, weights):
    real_part = spectrum[:, 0]
    imag_part = spectrum[:, 1]
    w_real = weights[:, :, 0]
    w_imag = weights[:, :, 1]
    out_real = product("ksim,mkio->ksom", real_part, w_real) - product(
        "ksim,mkio->ksom", imag_part, w_imag
    )
    out_imag = product("ksim,mkio->ksom", real_part, w_imag) + product(
        "ksim,mkio->ksom", imag_part, w_real
    )
    return jnp.stack([out_real, out_imag], axis=1).astype(jnp.bfloat16)


def spectral_pull(adjoint, weights):
    real_part = adjoint[:, 0]
    imag_part = adjoint[:, 1]
    w_real = weights[:, :, 0]
    w_imag = weights[:, :, 1]
    out_real = product("ksom,mkio->ksim", real_part, w_real) + product(
        "ksom,mkio->ksim", imag_part, w_imag
    )
    out_imag = product("ksom,mkio->ksim", imag_part, w_real) - product(
        "ksom,mkio->ksim", real_part, w_imag
    )
    return jnp.stack([out_real, out_imag], axis=1).astype(jnp.bfloat16)


def weight_grad(spectrum, adjoint):
    spec_real = spectrum[:, 0]
    spec_imag = spectrum[:, 1]
    adj_real = adjoint[:, 0]
    adj_imag = adjoint[:, 1]
    grad_real = product("ksim,ksom->mkio", spec_real, adj_real) + product(
        "ksim,ksom->mkio", spec_imag, adj_imag
    )
    grad_imag = product("ksim,ksom->mkio", spec_real, adj_imag) - product(
        "ksim,ksom->mkio", spec_imag, adj_real
    )
    return jnp.stack([grad_real, grad_imag], axis=2)


def to_modes(coarse):
    return lax.all_to_all(coarse, "space", split_axis=4, concat_axis=0, tiled=True)


def to_cells(returned):
    return lax.all_to_all(returned, "space", split_axis=0, concat_axis=4, tiled=True)


def plain_body(features, cotangent, spectral, pointwise, biases):
    samples, channels, slab_cells, span_y, span_z = features.shape
    full_length = slab_cells * lax.axis_size("space")
    plane_basis = plane_table(span_y, span_z, KY, KZ)
    line_basis = line_table(full_length, KX)
    doubling = mode_doubling(KY, KZ)
    doubling_cells = doubling.astype(jnp.bfloat16)[None, None, None, None, :]
    flat_cells = features.reshape(samples, channels, slab_cells, span_y * span_z)
    coarse = product("scxq,qmp->xpscm", flat_cells, plane_basis).astype(jnp.bfloat16)
    spectrum = forward_lines(to_modes(coarse), line_basis)
    local_modes = spectral.shape[0]
    blocks = lax.all_gather(spectral, "dp", axis=1, tiled=True)
    weights = blocks.reshape(local_modes, blocks.shape[1], 2, channels, channels)
    mixed_modes = spectral_mix(spectrum, weights)
    returned = to_cells(inverse_lines(mixed_modes, line_basis))
    spectral_part = product("xpscm,qmp->scxq", returned * doubling_cells, plane_basis)
    linear = product("sicq,io->socq", flat_cells, pointwise)
    pre_act = linear + biases.astype(jnp.float32)[None, :, None, None] + spectral_part
    upstream_grad = cotangent.reshape(flat_cells.shape).astype(jnp.float32)
    delta_cells = (upstream_grad * gelu_slope(pre_act)).astype(jnp.bfloat16)
    coarse_back = (
        product("scxq,qmp->xpscm", delta_cells, plane_basis) * doubling[None, None, None, None, :]
    ).astype(jnp.bfloat16)
    adjoint = forward_lines(to_modes(coarse_back), line_basis)
    pulled = spectral_pull(adjoint, weights)
    grad_terms = weight_grad(spectrum, adjoint)
    grad_spectral = lax.psum_scatter(
        grad_terms.reshape(local_modes, KX, 2 * channels * channels).astype(jnp.bfloat16),
        "dp",
        scatter_dimension=1,
        tiled=True,
    ).astype(jnp.float32)
    back_cells = to_cells(inverse_lines(pulled, line_basis))
    grad_cells = product("socq,io->sicq", delta_cells, pointwise) + product(
        "xpscm,qmp->scxq", back_cells, plane_basis
    )
    grad_input = grad_cells.astype(jnp.bfloat16).reshape(features.shape)
    return (grad_input, grad_spectral)


def np_frequencies(kept_count, length):
    indices = np.arange(kept_count)
    return np.where(indices < kept_count // 2, indices, indices + (length - kept_count))


def np_plane_rows(count_y, count_z, blocks, tiles, quads):
    turn_y = np.arange(count_y)[:, None] * np_frequencies(KY, count_y)[None, :] % count_y
    turn_z = np.arange(count_z)[:, None] * np.arange(KZ)[None, :] % count_z
    angles = 2.0 * np.pi * (
        turn_y[:, None, :, None] / count_y + turn_z[None, :, None, :] / count_z
    )
    factor = 1.0 / math.sqrt(count_y * count_z)
    table = np.stack([factor * np.cos(angles), -factor * np.sin(angles)], axis=0)
    table = table.reshape(2, count_y * count_z, blocks, tiles, quads)
    rows = table.transpose(4, 2, 0, 3, 1).reshape(-1, count_y * count_z)
    doubling = np.where(np.arange(KY * KZ) % KZ == 0, 1.0, 2.0).reshape(blocks, 1, tiles, quads)
    doubling = np.broadcast_to(doubling, (blocks, 2, tiles, quads)).transpose(3, 0, 1, 2)
    return rows.astype(ml_dtypes.bfloat16), doubling.reshape(-1, 1).astype(np.float32)


def np_line(full_length, blocks, owners):
    turns = np.arange(full_length)[:, None] * np_frequencies(KX, full_length)[None, :] % full_length
    angles = 2.0 * np.pi * turns / full_length
    factor = 1.0 / math.sqrt(full_length)
    cos_part, sine_part = factor * np.cos(angles), factor * np.sin(angles)
    table = np.stack(
        [np.stack([cos_part, -sine_part], 0), np.stack([sine_part, cos_part], 0)], 0
    )
    table = table.reshape(2, 2, blocks, full_length // blocks, owners, KX // owners)
    table = table.transpose(4, 1, 5, 2, 0, 3).reshape(2 * KX, 2 * full_length)
    return table.astype(ml_dtypes.bfloat16)


def np_selectors(channels, slab, quads):
    def one_hot(rows, columns, count_rows, count_columns):
        table = np.zeros((count_rows, count_columns), ml_dtypes.bfloat16)
        table[rows.reshape(-1), columns.reshape(-1)] = 1
        return table

    lanes = quads * channels
    j, c, x = np.meshgrid(np.arange(quads), np.arange(channels), np.arange(slab), indexing="ij")
    regroup = one_hot(
        (j * channels + c) * slab + x, (x * quads + j) * channels + c, lanes * slab, lanes * slab
    )
    j, i, o = np.meshgrid(
        np.arange(quads), np.arange(channels), np.arange(channels), indexing="ij"
    )
    spread = one_hot(
        j * channels + i,
        j * channels * channels + i * channels + o,
        lanes,
        quads * channels * channels,
    )
    spread = spread.reshape(lanes, quads, channels * channels).transpose(1, 0, 2)
    j, i, o = np.meshgrid(np.arange(quads), np.arange(quads), np.arange(channels), indexing="ij")
    tile = one_hot((j * quads + i) * channels + o, j * channels + o, quads * lanes, lanes)
    return regroup, np.ascontiguousarray(spread), tile


f32, bf16 = jnp.float32, jnp.bfloat16
NT = (((1,), (1,)), ((), ()))


def dot(left, right):
    return jnp.dot(left, right, preferred_element_type=f32)


def dot_nt(left, right):
    return lax.dot_general(left, right, NT, preferred_element_type=f32)


def start_exchange(axis, count, send, recv, send_sem, recv_sem):
    me = lax.axis_index(axis)
    copies = []
    for step in range(1, count):
        peer = lax.rem(me + step, count)
        copy = pltpu.make_async_remote_copy(
            src_ref=send.at[peer],
            dst_ref=recv.at[me],
            send_sem=send_sem.at[step],
            recv_sem=recv_sem.at[step],
            device_id={axis: peer},
            device_id_type=pl.DeviceIdType.MESH,
        )
        copy.start()
        copies.append(copy)
    recv[me] = send[me]
    return copies


def wait_all(copies):
    for copy in copies:
        copy.wait()


def layer_kernel(
    sizes,
    feats, cot, weights, mix_fwd, mix_back, bias, plane, doubling, line, regroup, spread, tile,
    out_input, out_spectral,
    coarse_acc, delta, spec_wide, adj_wide, cells, volume,
    space_send, space_recv, dp_send, dp_recv,
    space_ssem, space_rsem, dp_ssem, dp_rsem,
):
    blocks, owners, channels, slab, tiles, quads, kept = sizes
    lanes = quads * channels
    rows = 2 * kept * owners
    cells_count = feats.shape[1]
    chunk = 512
    chunks = cells_count // chunk
    group = blocks * 2 * 8
    mesh_id = pl.DeviceIdType.MESH

    barrier = pltpu.get_barrier_semaphore()
    for axis, count in (("space", blocks), ("dp", owners)):
        me = lax.axis_index(axis)
        for step in range(1, count):
            pl.semaphore_signal(
                barrier, inc=1, device_id={axis: lax.rem(me + step, count)}, device_id_type=mesh_id
            )
    pl.semaphore_wait(barrier, blocks + owners - 2)

    def send_cells(turn, coarse):
        wide = jnp.concatenate(
            [coarse[j * group : (j + 1) * group].astype(bf16) for j in range(quads)], axis=1
        )
        wide = dot(wide, regroup[...])
        for block in range(blocks):
            parts = [
                wide[(block * 2 + p) * 8 : (block * 2 + p + 1) * 8, x * lanes : (x + 1) * lanes]
                for p in range(2)
                for x in range(slab)
            ]
            space_send[turn, block] = jnp.concatenate(parts, axis=0).astype(bf16)
        return start_exchange(
            "space", blocks, space_send.at[turn], space_recv.at[turn],
            space_ssem.at[turn], space_rsem.at[turn],
        )

    def cells_to_modes(turn, dp_turn):
        cells[...] = space_recv[turn].astype(f32).reshape(cells.shape)
        count = blocks * 2 * slab
        for t in range(tiles):
            column = cells[pl.ds(t, count, stride=8), :].astype(bf16)
            spectrum = dot(line[...], column).astype(bf16)
            dp_send[dp_turn, :, :, t * lanes : (t + 1) * lanes] = spectrum.reshape(
                owners, 2 * kept, lanes
            )
        return start_dp(dp_turn)

    def start_dp(turn):
        return start_exchange(
            "dp", owners, dp_send.at[turn], dp_recv.at[turn], dp_ssem.at[turn], dp_rsem.at[turn]
        )

    def modes_to_cells(dp_turn, turn):
        count = blocks * 2 * slab
        for t in range(tiles):
            column = dp_recv[dp_turn, :, :, t * lanes : (t + 1) * lanes].reshape(rows, lanes)
            back = lax.dot_general(
                line[...], column, (((0,), (0,)), ((), ())), preferred_element_type=f32
            )
            cells[pl.ds(t, count, stride=8), :] = back
        space_send[turn] = cells[...].astype(bf16).reshape(space_send.shape[1:])
        return start_exchange(
            "space", blocks, space_send.at[turn], space_recv.at[turn],
            space_ssem.at[turn], space_rsem.at[turn],
        )

    def receive_volume(turn, scaled):
        parts = []
        for block in range(blocks):
            held = space_recv[turn, block].astype(f32)
            for p in range(2):
                parts.append(
                    jnp.concatenate(
                        [held[(p * slab + x) * 8 : (p * slab + x + 1) * 8] for x in range(slab)],
                        axis=1,
                    )
                )
        wide = jnp.concatenate(parts, axis=0).astype(bf16)
        wide = dot_nt(wide, regroup[...])
        for j in range(quads):
            part = wide[:, j * lanes : (j + 1) * lanes]
            if scaled:
                part = part * doubling[j * group : (j + 1) * group]
            volume[:, j * group : (j + 1) * group] = part.T.astype(bf16)

    coarse_acc[...] = jnp.zeros_like(coarse_acc)

    def analyse(step, _):
        at = pl.ds(pl.multiple_of(step * chunk, chunk), chunk)
        coarse_acc[...] += dot_nt(plane[:, at], feats[:, at])
        return 0

    lax.fori_loop(0, chunks, analyse, 0)
    wait_all(send_cells(0, coarse_acc[...]))
    wait_all(cells_to_modes(0, 0))

    def mix(t, _):
        at = pl.ds(pl.multiple_of(t * lanes, lanes), lanes)
        column = dp_recv[0, :, :, at].reshape(rows, lanes)
        parts = []
        for j in range(quads):
            m = t * quads + j
            spec_wide[m] = dot(column, spread[j])
            total = [None] * (2 * owners)
            for s in range(channels * channels // 128):
                lo = s * 128
                w_re = weights[m, :, lo : lo + 128].astype(f32)
                lo2 = channels * channels + lo
                w_im = weights[m, :, lo2 : lo2 + 128].astype(f32)
                for n in range(owners):
                    re = spec_wide[m, 2 * n * kept : (2 * n + 1) * kept, lo : lo + 128]
                    im = spec_wide[m, (2 * n + 1) * kept : (2 * n + 2) * kept, lo : lo + 128]
                    out_re = re * w_re - im * w_im
                    out_im = re * w_im + im * w_re
                    total[2 * n] = out_re if s == 0 else total[2 * n] + out_re
                    total[2 * n + 1] = out_im if s == 0 else total[2 * n + 1] + out_im
            parts.append(jnp.concatenate(total, axis=0).astype(bf16))
        mixed = dot(jnp.concatenate(parts, axis=1), tile[...])
        dp_send[1, :, :, at] = mixed.astype(bf16).reshape(owners, 2 * kept, lanes)
        return 0

    lax.fori_loop(0, tiles, mix, 0)
    wait_all(start_dp(1))
    wait_all(modes_to_cells(1, 1))
    receive_volume(1, True)

    coarse_acc[...] = jnp.zeros_like(coarse_acc)

    def activate(step, _):
        at = pl.ds(pl.multiple_of(step * chunk, chunk), chunk)
        pre_act = dot(volume[...], plane[:, at]) + dot(mix_fwd[...], feats[:, at]) + bias[...]
        part = (cot[:, at].astype(f32) * gelu_slope(pre_act)).astype(bf16)
        delta[:, at] = part
        coarse_acc[...] += dot_nt(plane[:, at], part)
        return 0

    lax.fori_loop(0, chunks, activate, 0)
    wait_all(send_cells(2, coarse_acc[...] * doubling[...]))
    wait_all(cells_to_modes(2, 2))

    def pull(t, _):
        at = pl.ds(pl.multiple_of(t * lanes, lanes), lanes)
        column = dp_recv[2, :, :, at].reshape(rows, lanes)
        pulled = jnp.zeros((rows, lanes), f32)
        for j in range(quads):
            m = t * quads + j
            wide = dot_nt(column, tile[j * lanes : (j + 1) * lanes])
            adj_wide[m] = wide
            adjs = [wide[r * kept : (r + 1) * kept] for r in range(2 * owners)]
            products = []
            for s in range(channels * channels // 128):
                lo = s * 128
                w_re = weights[m, :, lo : lo + 128].astype(f32)
                lo2 = channels * channels + lo
                w_im = weights[m, :, lo2 : lo2 + 128].astype(f32)
                terms = []
                for n in range(owners):
                    re, im = adjs[2 * n], adjs[2 * n + 1]
                    terms += [re * w_re + im * w_im, im * w_re - re * w_im]
                products.append(jnp.concatenate(terms, axis=0).astype(bf16))
            pulled += dot_nt(jnp.concatenate(products, axis=1), spread[j])
        dp_send[3, :, :, at] = pulled.astype(bf16).reshape(owners, 2 * kept, lanes)
        return 0

    lax.fori_loop(0, tiles, pull, 0)
    copies = start_dp(3)

    def weight_terms(m, _):
        adjs = [adj_wide[m, r * kept : (r + 1) * kept] for r in range(2 * owners)]
        for s in range(channels * channels // 128):
            lo = s * 128
            grad_re, grad_im = None, None
            for n in range(owners):
                re = spec_wide[m, 2 * n * kept : (2 * n + 1) * kept, lo : lo + 128]
                im = spec_wide[m, (2 * n + 1) * kept : (2 * n + 2) * kept, lo : lo + 128]
                a_re, a_im = adjs[2 * n], adjs[2 * n + 1]
                term_re = re * a_re + im * a_im
                term_im = re * a_im - im * a_re
                grad_re = term_re if n == 0 else grad_re + term_re
                grad_im = term_im if n == 0 else grad_im + term_im
            out_spectral[m, :, lo : lo + 128] = grad_re
            lo2 = channels * channels + lo
            out_spectral[m, :, lo2 : lo2 + 128] = grad_im
        return 0

    lax.fori_loop(0, tiles * quads, weight_terms, 0)
    wait_all(copies)
    wait_all(modes_to_cells(3, 3))
    receive_volume(3, False)

    def finish(step, _):
        at = pl.ds(pl.multiple_of(step * chunk, chunk), chunk)
        grad = dot(volume[...], plane[:, at]) + dot(mix_back[...], delta[:, at])
        out_input[:, at] = grad.astype(bf16)
        return 0

    lax.fori_loop(0, chunks, finish, 0)


def fits(features, spectral, owners):
    samples, channels, slab = features.shape[:3]
    modes, kept = spectral.shape[:2]
    return (
        samples == 1 and kept == 8 and channels == 32 and slab == 4
        and modes == 32 and (2 * kept * owners) % 16 == 0
    )


def body(features, cotangent, spectral, pointwise, biases):
    blocks, owners = lax.axis_size("space"), lax.axis_size("dp")
    if not fits(features, spectral, owners):
        return plain_body(features, cotangent, spectral, pointwise, biases)
    _, channels, slab, span_y, span_z = features.shape
    modes, kept = spectral.shape[:2]
    tiles = 8
    quads = modes // tiles
    lanes = quads * channels
    cell_rows, cells_count = channels * slab, span_y * span_z
    plane, doubling = np_plane_rows(span_y, span_z, blocks, tiles, quads)
    line = np_line(slab * blocks, blocks, owners)
    regroup, spread, tile = np_selectors(channels, slab, quads)
    eye = jnp.eye(slab, dtype=bf16)
    mix_back = jnp.einsum("io,xy->ixoy", pointwise, eye).reshape(cell_rows, cell_rows)
    mix_fwd = jnp.einsum("io,xy->oxiy", pointwise, eye).reshape(cell_rows, cell_rows)
    bias = jnp.repeat(biases.astype(f32), slab)[:, None]
    plane_rows = plane.shape[0]
    sizes = (blocks, owners, channels, slab, tiles, quads, kept)
    vmem = pl.BlockSpec(memory_space=pltpu.VMEM)
    grad_input, grad_spectral = pl.pallas_call(
        functools.partial(layer_kernel, sizes),
        out_shape=(
            jax.ShapeDtypeStruct((cell_rows, cells_count), bf16),
            jax.ShapeDtypeStruct(spectral.shape, f32),
        ),
        in_specs=[vmem] * 12,
        out_specs=(vmem, vmem),
        scratch_shapes=[
            pltpu.VMEM((plane_rows, cell_rows), f32),
            pltpu.VMEM((cell_rows, cells_count), bf16),
            pltpu.VMEM((modes, 2 * kept * owners, channels * channels), f32),
            pltpu.VMEM((modes, 2 * kept * owners, 128), f32),
            pltpu.VMEM((blocks * 2 * slab * 8, lanes), f32),
            pltpu.VMEM((cell_rows, plane_rows), bf16),
            pltpu.VMEM((4, blocks, 2 * slab * 8, lanes), bf16),
            pltpu.VMEM((4, blocks, 2 * slab * 8, lanes), bf16),
            pltpu.VMEM((4, owners, 2 * kept, modes * channels), bf16),
            pltpu.VMEM((4, owners, 2 * kept, modes * channels), bf16),
            pltpu.SemaphoreType.DMA((4, blocks)),
            pltpu.SemaphoreType.DMA((4, blocks)),
            pltpu.SemaphoreType.DMA((4, owners)),
            pltpu.SemaphoreType.DMA((4, owners)),
        ],
        compiler_params=pltpu.CompilerParams(
            collective_id=0, has_side_effects=True, vmem_limit_bytes=56 * 1024 * 1024
        ),
    )(
        features.reshape(cell_rows, cells_count),
        cotangent.reshape(cell_rows, cells_count),
        spectral, mix_fwd, mix_back, bias,
        plane, doubling, line, regroup, spread, tile,
    )
    return grad_input.reshape(features.shape), grad_spectral


def solution(mesh):
    placed = (
        P("dp", None, "space", None, None),
        P("dp", None, "space", None, None),
        P("space", "dp", None),
        P(),
        P(),
    )
    return jax.shard_map(
        body,
        mesh=mesh,
        in_specs=placed,
        out_specs=(P("dp", None, "space", None, None), P("space", "dp", None)),
        check_vma=False,
    )
```

```python
import functools
import math

import jax
import jax.numpy as jnp
import ml_dtypes
import numpy as np
from jax import lax
from jax.experimental import pallas as pl
from jax.experimental.pallas import tpu as pltpu
from jax.sharding import PartitionSpec as P

KX = 32
KY = 32
KZ = 8


tanh_coef = 0.7978845608028654
cubic_coef = 0.044715


def frequencies(kept_count, length):
    indices = jnp.arange(kept_count, dtype=jnp.int32)
    return jnp.where(indices < kept_count // 2, indices, indices + (length - kept_count))


def plane_table(count_y, count_z, kept_y, kept_z):
    freq_y = frequencies(kept_y, count_y)
    freq_z = jnp.arange(kept_z, dtype=jnp.int32)
    turn_y = jnp.arange(count_y, dtype=jnp.int32)[:, None] * freq_y[None, :] % count_y
    turn_z = jnp.arange(count_z, dtype=jnp.int32)[:, None] * freq_z[None, :] % count_z
    angles = (
        2.0
        * math.pi
        * (
            turn_y[:, None, :, None].astype(jnp.float32) / count_y
            + turn_z[None, :, None, :].astype(jnp.float32) / count_z
        )
    )
    factor = 1.0 / math.sqrt(count_y * count_z)
    basis_table = jnp.stack([factor * jnp.cos(angles), -factor * jnp.sin(angles)], axis=-1)
    return basis_table.reshape(count_y * count_z, kept_y * kept_z, 2).astype(jnp.bfloat16)


def line_table(full_length, kept_count):
    freq_x = frequencies(kept_count, full_length)
    turns = jnp.arange(full_length, dtype=jnp.int32)[:, None] * freq_x[None, :] % full_length
    angles = 2.0 * math.pi * turns.astype(jnp.float32) / full_length
    factor = 1.0 / math.sqrt(full_length)
    cos_part = factor * jnp.cos(angles)
    sine_part = factor * jnp.sin(angles)
    first_row = jnp.stack([cos_part, -sine_part], axis=1)
    second = jnp.stack([sine_part, cos_part], axis=1)
    return jnp.stack([first_row, second], axis=0).astype(jnp.bfloat16)


def mode_doubling(kept_y, kept_z):
    mode_index = jnp.arange(kept_y * kept_z, dtype=jnp.int32) % kept_z
    return jnp.where(mode_index == 0, 1.0, 2.0).astype(jnp.float32)


def gelu_slope(values):
    inner_arg = tanh_coef * (values + cubic_coef * values * values * values)
    tanh_part = jnp.tanh(inner_arg)
    return 0.5 * (1.0 + tanh_part) + 0.5 * values * (1.0 - tanh_part * tanh_part) * tanh_coef * (
        1.0 + 3.0 * cubic_coef * values * values
    )


def product(equation, left_op, right_op):
    return jnp.einsum(equation, left_op, right_op, preferred_element_type=jnp.float32)


def forward_lines(coarse, line_basis):
    return product("xpscm,pxqk->kqscm", coarse, line_basis).astype(jnp.bfloat16)


def inverse_lines(spectrum, line_basis):
    return product("kqscm,pxqk->xpscm", spectrum, line_basis).astype(jnp.bfloat16)


def spectral_mix(spectrum, weights):
    real_part = spectrum[:, 0]
    imag_part = spectrum[:, 1]
    w_real = weights[:, :, 0]
    w_imag = weights[:, :, 1]
    out_real = product("ksim,mkio->ksom", real_part, w_real) - product(
        "ksim,mkio->ksom", imag_part, w_imag
    )
    out_imag = product("ksim,mkio->ksom", real_part, w_imag) + product(
        "ksim,mkio->ksom", imag_part, w_real
    )
    return jnp.stack([out_real, out_imag], axis=1).astype(jnp.bfloat16)


def spectral_pull(adjoint, weights):
    real_part = adjoint[:, 0]
    imag_part = adjoint[:, 1]
    w_real = weights[:, :, 0]
    w_imag = weights[:, :, 1]
    out_real = product("ksom,mkio->ksim", real_part, w_real) + product(
        "ksom,mkio->ksim", imag_part, w_imag
    )
    out_imag = product("ksom,mkio->ksim", imag_part, w_real) - product(
        "ksom,mkio->ksim", real_part, w_imag
    )
    return jnp.stack([out_real, out_imag], axis=1).astype(jnp.bfloat16)


def weight_grad(spectrum, adjoint):
    spec_real = spectrum[:, 0]
    spec_imag = spectrum[:, 1]
    adj_real = adjoint[:, 0]
    adj_imag = adjoint[:, 1]
    grad_real = product("ksim,ksom->mkio", spec_real, adj_real) + product(
        "ksim,ksom->mkio", spec_imag, adj_imag
    )
    grad_imag = product("ksim,ksom->mkio", spec_real, adj_imag) - product(
        "ksim,ksom->mkio", spec_imag, adj_real
    )
    return jnp.stack([grad_real, grad_imag], axis=2)


def to_modes(coarse):
    return lax.all_to_all(coarse, "space", split_axis=4, concat_axis=0, tiled=True)


def to_cells(returned):
    return lax.all_to_all(returned, "space", split_axis=0, concat_axis=4, tiled=True)


def plain_body(features, cotangent, spectral, pointwise, biases):
    samples, channels, slab_cells, span_y, span_z = features.shape
    full_length = slab_cells * lax.axis_size("space")
    plane_basis = plane_table(span_y, span_z, KY, KZ)
    line_basis = line_table(full_length, KX)
    doubling = mode_doubling(KY, KZ)
    doubling_cells = doubling.astype(jnp.bfloat16)[None, None, None, None, :]
    flat_cells = features.reshape(samples, channels, slab_cells, span_y * span_z)
    coarse = product("scxq,qmp->xpscm", flat_cells, plane_basis).astype(jnp.bfloat16)
    spectrum = forward_lines(to_modes(coarse), line_basis)
    local_modes = spectral.shape[0]
    blocks = lax.all_gather(spectral, "dp", axis=1, tiled=True)
    weights = blocks.reshape(local_modes, blocks.shape[1], 2, channels, channels)
    mixed_modes = spectral_mix(spectrum, weights)
    returned = to_cells(inverse_lines(mixed_modes, line_basis))
    spectral_part = product("xpscm,qmp->scxq", returned * doubling_cells, plane_basis)
    linear = product("sicq,io->socq", flat_cells, pointwise)
    pre_act = linear + biases.astype(jnp.float32)[None, :, None, None] + spectral_part
    upstream_grad = cotangent.reshape(flat_cells.shape).astype(jnp.float32)
    delta_cells = (upstream_grad * gelu_slope(pre_act)).astype(jnp.bfloat16)
    coarse_back = (
        product("scxq,qmp->xpscm", delta_cells, plane_basis) * doubling[None, None, None, None, :]
    ).astype(jnp.bfloat16)
    adjoint = forward_lines(to_modes(coarse_back), line_basis)
    pulled = spectral_pull(adjoint, weights)
    grad_terms = weight_grad(spectrum, adjoint)
    grad_spectral = lax.psum_scatter(
        grad_terms.reshape(local_modes, KX, 2 * channels * channels).astype(jnp.bfloat16),
        "dp",
        scatter_dimension=1,
        tiled=True,
    ).astype(jnp.float32)
    back_cells = to_cells(inverse_lines(pulled, line_basis))
    grad_cells = product("socq,io->sicq", delta_cells, pointwise) + product(
        "xpscm,qmp->scxq", back_cells, plane_basis
    )
    grad_input = grad_cells.astype(jnp.bfloat16).reshape(features.shape)
    return (grad_input, grad_spectral)


def np_frequencies(kept_count, length):
    indices = np.arange(kept_count)
    return np.where(indices < kept_count // 2, indices, indices + (length - kept_count))


def np_plane_rows(count_y, count_z, blocks, tiles, quads):
    turn_y = np.arange(count_y)[:, None] * np_frequencies(KY, count_y)[None, :] % count_y
    turn_z = np.arange(count_z)[:, None] * np.arange(KZ)[None, :] % count_z
    angles = 2.0 * np.pi * (
        turn_y[:, None, :, None] / count_y + turn_z[None, :, None, :] / count_z
    )
    factor = 1.0 / math.sqrt(count_y * count_z)
    table = np.stack([factor * np.cos(angles), -factor * np.sin(angles)], axis=0)
    table = table.reshape(2, count_y * count_z, blocks, tiles, quads)
    rows = table.transpose(4, 2, 0, 3, 1).reshape(-1, count_y * count_z)
    doubling = np.where(np.arange(KY * KZ) % KZ == 0, 1.0, 2.0).reshape(blocks, 1, tiles, quads)
    doubling = np.broadcast_to(doubling, (blocks, 2, tiles, quads)).transpose(3, 0, 1, 2)
    return rows.astype(ml_dtypes.bfloat16), doubling.reshape(-1, 1).astype(np.float32)


def np_line(full_length, blocks, owners):
    turns = np.arange(full_length)[:, None] * np_frequencies(KX, full_length)[None, :] % full_length
    angles = 2.0 * np.pi * turns / full_length
    factor = 1.0 / math.sqrt(full_length)
    cos_part, sine_part = factor * np.cos(angles), factor * np.sin(angles)
    table = np.stack(
        [np.stack([cos_part, -sine_part], 0), np.stack([sine_part, cos_part], 0)], 0
    )
    table = table.reshape(2, 2, blocks, full_length // blocks, owners, KX // owners)
    table = table.transpose(4, 1, 5, 2, 0, 3).reshape(2 * KX, 2 * full_length)
    return table.astype(ml_dtypes.bfloat16)


def np_selectors(channels, slab, quads):
    def one_hot(rows, columns, count_rows, count_columns):
        table = np.zeros((count_rows, count_columns), ml_dtypes.bfloat16)
        table[rows.reshape(-1), columns.reshape(-1)] = 1
        return table

    lanes = quads * channels
    j, c, x = np.meshgrid(np.arange(quads), np.arange(channels), np.arange(slab), indexing="ij")
    regroup = one_hot(
        (j * channels + c) * slab + x, (x * quads + j) * channels + c, lanes * slab, lanes * slab
    )
    j, i, o = np.meshgrid(
        np.arange(quads), np.arange(channels), np.arange(channels), indexing="ij"
    )
    spread = one_hot(
        j * channels + i,
        j * channels * channels + i * channels + o,
        lanes,
        quads * channels * channels,
    )
    spread = spread.reshape(lanes, quads, channels * channels).transpose(1, 0, 2)
    j, i, o = np.meshgrid(np.arange(quads), np.arange(quads), np.arange(channels), indexing="ij")
    tile = one_hot((j * quads + i) * channels + o, j * channels + o, quads * lanes, lanes)
    cells = np.arange(channels * slab)
    repeat = one_hot(cells, cells // slab, channels * slab, channels)
    flat = np.ascontiguousarray
    return regroup, flat(spread), flat(spread.transpose(0, 2, 1)), tile, flat(tile.T), repeat


f32, bf16 = jnp.float32, jnp.bfloat16
NT = (((1,), (1,)), ((), ()))
TN = (((0,), (0,)), ((), ()))
HALVES = 2


def dot(left, right):
    return jnp.dot(left, right, preferred_element_type=f32)


def dot_nt(left, right):
    return lax.dot_general(left, right, NT, preferred_element_type=f32)


def start_exchange(axis, count, send, recv, send_sem, recv_sem):
    me = lax.axis_index(axis)
    copies = []
    for step in range(1, count):
        peer = lax.rem(me + step, count)
        copy = pltpu.make_async_remote_copy(
            src_ref=send.at[peer],
            dst_ref=recv.at[me],
            send_sem=send_sem.at[step],
            recv_sem=recv_sem.at[step],
            device_id={axis: peer},
            device_id_type=pl.DeviceIdType.MESH,
        )
        copy.start()
        copies.append(copy)
    recv[me] = send[me]
    return copies


def wait_all(copies):
    for copy in copies:
        copy.wait()


def layer_kernel(
    sizes,
    feats, cot_hbm, weights_hbm, pointwise, biases, analysis_hbm, synthesis_hbm,
    doubling, line, regroup, spread, gather, tile, untile, repeat,
    out_input, out_spectral,
    cot, weights, analysis, synthesis, grads,
    natural, rows_in, delta, coarse_acc, volume, mix_fwd, mix_back, bias,
    stack, parts, spec_wide, adj_wide, products, pulled, cells,
    space_send, space_recv, dp_send, dp_recv,
    load_sem, analysis_sem, space_ssem, space_rsem, dp_ssem, dp_rsem,
):
    blocks, owners, channels, slab, span_y, tiles, quads, kept = sizes
    lanes = quads * channels
    rows = 2 * kept * owners
    cell_rows = channels * slab
    width = feats.shape[1]
    cells_count = span_y * width
    chunk = analysis_hbm.shape[0] // analysis_sem.shape[0]
    chunks = cells_count // chunk
    lines = chunk // width
    group = blocks * 2 * tiles
    near = tiles // HALVES
    square = channels * channels
    mesh_id = pl.DeviceIdType.MESH

    analysis_loads = [
        pltpu.make_async_copy(
            analysis_hbm.at[pl.ds(step * chunk, chunk)],
            analysis.at[pl.ds(step * chunk, chunk)],
            analysis_sem.at[step],
        )
        for step in range(chunks)
    ]
    for copy in analysis_loads:
        copy.start()
    load_cot = pltpu.make_async_copy(cot_hbm, cot, load_sem.at[0])
    load_weights = pltpu.make_async_copy(weights_hbm, weights, load_sem.at[1])
    load_synthesis = pltpu.make_async_copy(synthesis_hbm, synthesis, load_sem.at[2])
    load_cot.start()
    load_weights.start()
    load_synthesis.start()

    barrier = pltpu.get_barrier_semaphore()
    for axis, count in (("space", blocks), ("dp", owners)):
        me = lax.axis_index(axis)
        for step in range(1, count):
            pl.semaphore_signal(
                barrier, inc=1, device_id={axis: lax.rem(me + step, count)}, device_id_type=mesh_id
            )

    def widen(source):
        def some(step, _):
            at = pl.ds(pl.multiple_of(step * 512, 512), 512)
            natural[at, :] = source[at, :].astype(f32)
            return 0

        lax.fori_loop(0, natural.shape[0] // 512, some, 0)

    def plane_lines(step):
        return jnp.concatenate(
            [natural[pl.ds(step * lines + u, cell_rows, stride=span_y), :] for u in range(lines)],
            axis=1,
        )

    def columns(step):
        return pl.ds(pl.multiple_of(step * chunk, chunk), chunk)

    def send_space(turn):
        return start_exchange(
            "space", blocks, space_send.at[turn], space_recv.at[turn],
            space_ssem.at[turn], space_rsem.at[turn],
        )

    def send_dp(turn, half):
        at = turn * HALVES + half
        return start_exchange(
            "dp", owners, dp_send.at[at], dp_recv.at[at], dp_ssem.at[at], dp_rsem.at[at]
        )

    def send_cells(turn, coarse):
        wide = jnp.concatenate(
            [coarse[:, j * group : (j + 1) * group].T.astype(bf16) for j in range(quads)], axis=1
        )
        wide = dot(wide, regroup[...])
        for block in range(blocks):
            pieces = [
                wide[
                    (block * 2 + p) * tiles : (block * 2 + p + 1) * tiles,
                    x * lanes : (x + 1) * lanes,
                ]
                for p in range(2)
                for x in range(slab)
            ]
            space_send[turn, block] = jnp.concatenate(pieces, axis=0).astype(bf16)
        return send_space(turn)

    def cells_to_modes(turn, dp_turn):
        cells[...] = space_recv[turn].astype(f32).reshape(cells.shape)
        copies = []
        for half in range(HALVES):
            wide = jnp.concatenate(
                [
                    cells[pl.ds(half * near + t, blocks * 2 * slab, stride=tiles), :]
                    for t in range(near)
                ],
                axis=1,
            ).astype(bf16)
            spectrum = dot(line[...], wide).astype(bf16)
            dp_send[dp_turn * HALVES + half] = spectrum.reshape(owners, 2 * kept, near * lanes)
            copies.append(send_dp(dp_turn, half))
        return copies

    def modes_to_cells(dp_turn, turn, copies):
        for half in range(HALVES):
            wait_all(copies[half])
            wide = dp_recv[dp_turn * HALVES + half].reshape(rows, near * lanes)
            back = lax.dot_general(line[...], wide, TN, preferred_element_type=f32)
            for t in range(near):
                cells[pl.ds(half * near + t, blocks * 2 * slab, stride=tiles), :] = back[
                    :, t * lanes : (t + 1) * lanes
                ]
        space_send[turn] = cells[...].astype(bf16).reshape(space_send.shape[1:])
        return send_space(turn)

    def receive_volume(turn, scaled):
        pieces = []
        for block in range(blocks):
            held = space_recv[turn, block].astype(f32)
            for p in range(2):
                pieces.append(
                    jnp.concatenate(
                        [
                            held[(p * slab + x) * tiles : (p * slab + x + 1) * tiles]
                            for x in range(slab)
                        ],
                        axis=1,
                    )
                )
        wide = dot_nt(jnp.concatenate(pieces, axis=0).astype(bf16), regroup[...])
        for j in range(quads):
            part = wide[:, j * lanes : (j + 1) * lanes].T
            if scaled:
                part = part * doubling[:, j * group : (j + 1) * group]
            volume[:, j * group : (j + 1) * group] = part.astype(bf16)

    def stack_half(dp_turn, half):
        for t in range(near):
            stack[t * rows : (t + 1) * rows] = dp_recv[
                dp_turn * HALVES + half, :, :, t * lanes : (t + 1) * lanes
            ].reshape(rows, lanes)

    def unstack_half(dp_turn, half, values):
        for t in range(near):
            dp_send[dp_turn * HALVES + half, :, :, t * lanes : (t + 1) * lanes] = (
                values[t * rows : (t + 1) * rows].astype(bf16).reshape(owners, 2 * kept, lanes)
            )
        return send_dp(dp_turn, half)

    def weight_tiles(m, s):
        lo = s * 128
        return (
            weights[m, :, lo : lo + 128].astype(f32),
            weights[m, :, square + lo : square + lo + 128].astype(f32),
        )

    widen(feats)
    coarse_acc[...] = jnp.zeros_like(coarse_acc)
    for step in range(chunks):
        analysis_loads[step].wait()
        part = plane_lines(step).astype(bf16)
        rows_in[:, step * chunk : (step + 1) * chunk] = part
        coarse_acc[...] += dot(part, analysis[step * chunk : (step + 1) * chunk, :])
    pl.semaphore_wait(barrier, blocks + owners - 2)
    copies = send_cells(0, coarse_acc[...])

    same_cell = lax.rem(lax.broadcasted_iota(jnp.int32, mix_fwd.shape, 0), slab) == lax.rem(
        lax.broadcasted_iota(jnp.int32, mix_fwd.shape, 1), slab
    )
    spread_out = dot_nt(dot_nt(repeat[...], pointwise[...]).astype(bf16), repeat[...])
    mix_fwd[...] = jnp.where(same_cell, spread_out, 0.0).astype(bf16)
    spread_out = dot_nt(dot(repeat[...], pointwise[...]).astype(bf16), repeat[...])
    mix_back[...] = jnp.where(same_cell, spread_out, 0.0).astype(bf16)
    bias[...] = jnp.sum(
        repeat[...].astype(f32) * biases[...].astype(f32), axis=1, keepdims=True
    )
    load_cot.wait()
    widen(cot)
    wait_all(copies)
    copies = cells_to_modes(0, 0)
    load_weights.wait()

    back_copies = []
    for half in range(HALVES):
        wait_all(copies[half])
        stack_half(0, half)

        def mix(j, _, half=half):
            spec_wide[half, j] = dot(stack[...], spread[j])
            for t in range(near):
                m = (half * near + t) * quads + j
                base = t * rows
                total = [None] * (2 * owners)
                for s in range(square // 128):
                    lo = s * 128
                    w_re, w_im = weight_tiles(m, s)
                    for n in range(owners):
                        at = base + 2 * n * kept
                        re = spec_wide[half, j, at : at + kept, lo : lo + 128]
                        im = spec_wide[half, j, at + kept : at + 2 * kept, lo : lo + 128]
                        out_re = re * w_re - im * w_im
                        out_im = re * w_im + im * w_re
                        total[2 * n] = out_re if s == 0 else total[2 * n] + out_re
                        total[2 * n + 1] = out_im if s == 0 else total[2 * n + 1] + out_im
                parts[j, base : base + rows, :] = jnp.concatenate(total, axis=0).astype(bf16)
            return 0

        lax.fori_loop(0, quads, mix, 0)
        mixed = dot(jnp.concatenate([parts[j] for j in range(quads)], axis=1), tile[...])
        back_copies.append(unstack_half(1, half, mixed))
    wait_all(modes_to_cells(1, 1, back_copies))
    load_synthesis.wait()
    receive_volume(1, True)

    coarse_acc[...] = jnp.zeros_like(coarse_acc)

    def activate(step, _):
        at = columns(step)
        pre_act = dot(volume[...], synthesis[:, at]) + dot(mix_fwd[...], rows_in[:, at]) + bias[...]
        part = (plane_lines(step) * gelu_slope(pre_act)).astype(bf16)
        delta[:, at] = part
        coarse_acc[...] += dot(part, analysis[at, :])
        return 0

    lax.fori_loop(0, chunks, activate, 0)
    wait_all(send_cells(2, coarse_acc[...] * doubling[...]))
    copies = cells_to_modes(2, 2)

    back_copies = []
    for half in range(HALVES):
        wait_all(copies[half])
        stack_half(2, half)
        wide = dot(stack[...], untile[...])
        for j in range(quads):
            adj_wide[half, j] = wide[:, j * lanes : (j + 1) * lanes]
        pulled[...] = jnp.zeros_like(pulled)

        def pull(j, _, half=half):
            for t in range(near):
                m = (half * near + t) * quads + j
                base = t * rows
                adjs = [
                    adj_wide[half, j, base + r * kept : base + (r + 1) * kept]
                    for r in range(2 * owners)
                ]
                for s in range(square // 128):
                    w_re, w_im = weight_tiles(m, s)
                    terms = []
                    for n in range(owners):
                        re, im = adjs[2 * n], adjs[2 * n + 1]
                        terms += [re * w_re + im * w_im, im * w_re - re * w_im]
                    products[base : base + rows, s * 128 : (s + 1) * 128] = jnp.concatenate(
                        terms, axis=0
                    ).astype(bf16)
            pulled[...] += dot(products[...], gather[j])
            return 0

        lax.fori_loop(0, quads, pull, 0)
        back_copies.append(unstack_half(3, half, pulled[...]))

    for half in range(HALVES):

        def weight_terms(j, _, half=half):
            for t in range(near):
                m = (half * near + t) * quads + j
                base = t * rows
                adjs = [
                    adj_wide[half, j, base + r * kept : base + (r + 1) * kept]
                    for r in range(2 * owners)
                ]
                for s in range(square // 128):
                    lo = s * 128
                    grad_re, grad_im = None, None
                    for n in range(owners):
                        at = base + 2 * n * kept
                        re = spec_wide[half, j, at : at + kept, lo : lo + 128]
                        im = spec_wide[half, j, at + kept : at + 2 * kept, lo : lo + 128]
                        a_re, a_im = adjs[2 * n], adjs[2 * n + 1]
                        term_re = re * a_re + im * a_im
                        term_im = re * a_im - im * a_re
                        grad_re = term_re if n == 0 else grad_re + term_re
                        grad_im = term_im if n == 0 else grad_im + term_im
                    grads[m, :, lo : lo + 128] = grad_re
                    grads[m, :, square + lo : square + lo + 128] = grad_im
            return 0

        lax.fori_loop(0, quads, weight_terms, 0)
    store_grads = pltpu.make_async_copy(grads, out_spectral, load_sem.at[3])
    store_grads.start()
    wait_all(modes_to_cells(3, 3, back_copies))
    receive_volume(3, False)

    def finish(step, _):
        at = columns(step)
        grad = dot(volume[...], synthesis[:, at]) + dot(mix_back[...], delta[:, at])
        for u in range(lines):
            natural[pl.ds(step * lines + u, cell_rows, stride=span_y), :] = grad[
                :, u * width : (u + 1) * width
            ]
        return 0

    lax.fori_loop(0, chunks, finish, 0)

    def narrow(step, _):
        at = pl.ds(pl.multiple_of(step * 512, 512), 512)
        out_input[at, :] = natural[at, :].astype(bf16)
        return 0

    lax.fori_loop(0, natural.shape[0] // 512, narrow, 0)
    store_grads.wait()


def fits(features, spectral, owners):
    samples, channels, slab, span_y, span_z = features.shape
    modes, kept = spectral.shape[:2]
    return (
        samples == 1 and kept == 8 and channels == 32 and slab == 4 and modes == 32
        and span_z == 128 and span_y % 8 == 0 and (2 * kept * owners) % 16 == 0
    )


def body(features, cotangent, spectral, pointwise, biases):
    blocks, owners = lax.axis_size("space"), lax.axis_size("dp")
    if not fits(features, spectral, owners):
        return plain_body(features, cotangent, spectral, pointwise, biases)
    _, channels, slab, span_y, span_z = features.shape
    modes, kept = spectral.shape[:2]
    tiles = 8
    quads = modes // tiles
    lanes = quads * channels
    square = channels * channels
    cell_rows, cells_count = channels * slab, span_y * span_z
    natural_shape = (cell_rows * span_y, span_z)
    plane, doubling = np_plane_rows(span_y, span_z, blocks, tiles, quads)
    line = np_line(slab * blocks, blocks, owners)
    selectors = np_selectors(channels, slab, quads)
    plane_rows = plane.shape[0]
    chunks = 8
    rows = 2 * kept * owners
    half_rows = rows * tiles // HALVES
    sizes = (blocks, owners, channels, slab, span_y, tiles, quads, kept)
    vmem = pl.BlockSpec(memory_space=pltpu.VMEM)
    hbm = pl.BlockSpec(memory_space=pl.ANY)
    space_shape = (4, blocks, 2 * slab * tiles, lanes)
    dp_shape = (4 * HALVES, owners, 2 * kept, tiles // HALVES * lanes)
    grad_input, grad_spectral = pl.pallas_call(
        functools.partial(layer_kernel, sizes),
        out_shape=(
            jax.ShapeDtypeStruct(natural_shape, bf16),
            jax.ShapeDtypeStruct(spectral.shape, f32),
        ),
        in_specs=[vmem, hbm, hbm, vmem, vmem, hbm, hbm] + [vmem] * 8,
        out_specs=(vmem, hbm),
        scratch_shapes=[
            pltpu.VMEM(natural_shape, bf16),
            pltpu.VMEM(spectral.shape, bf16),
            pltpu.VMEM((cells_count, plane_rows), bf16),
            pltpu.VMEM((plane_rows, cells_count), bf16),
            pltpu.VMEM(spectral.shape, f32),
            pltpu.VMEM(natural_shape, f32),
            pltpu.VMEM((cell_rows, cells_count), bf16),
            pltpu.VMEM((cell_rows, cells_count), bf16),
            pltpu.VMEM((cell_rows, plane_rows), f32),
            pltpu.VMEM((cell_rows, plane_rows), bf16),
            pltpu.VMEM((cell_rows, cell_rows), bf16),
            pltpu.VMEM((cell_rows, cell_rows), bf16),
            pltpu.VMEM((cell_rows, 1), f32),
            pltpu.VMEM((half_rows, lanes), bf16),
            pltpu.VMEM((quads, half_rows, lanes), bf16),
            pltpu.VMEM((HALVES, quads, half_rows, square), f32),
            pltpu.VMEM((HALVES, quads, half_rows, lanes), f32),
            pltpu.VMEM((half_rows, square), bf16),
            pltpu.VMEM((half_rows, lanes), f32),
            pltpu.VMEM((blocks * 2 * slab * tiles, lanes), f32),
            pltpu.VMEM(space_shape, bf16),
            pltpu.VMEM(space_shape, bf16),
            pltpu.VMEM(dp_shape, bf16),
            pltpu.VMEM(dp_shape, bf16),
            pltpu.SemaphoreType.DMA((4,)),
            pltpu.SemaphoreType.DMA((chunks,)),
            pltpu.SemaphoreType.DMA((4, blocks)),
            pltpu.SemaphoreType.DMA((4, blocks)),
            pltpu.SemaphoreType.DMA((4 * HALVES, owners)),
            pltpu.SemaphoreType.DMA((4 * HALVES, owners)),
        ],
        compiler_params=pltpu.CompilerParams(
            collective_id=0, has_side_effects=True, vmem_limit_bytes=56 * 1024 * 1024
        ),
    )(
        features.reshape(natural_shape),
        cotangent.reshape(natural_shape),
        spectral, pointwise, biases[None, :],
        np.ascontiguousarray(plane.T), plane, doubling.T, line, *selectors,
    )
    return grad_input.reshape(features.shape), grad_spectral


def solution(mesh):
    placed = (
        P("dp", None, "space", None, None),
        P("dp", None, "space", None, None),
        P("space", "dp", None),
        P(),
        P(),
    )
    return jax.shard_map(
        body,
        mesh=mesh,
        in_specs=placed,
        out_specs=(P("dp", None, "space", None, None), P("space", "dp", None)),
        check_vma=False,
    )
```

```python
import functools
import math

import jax
import jax.numpy as jnp
import ml_dtypes
import numpy as np
from jax import lax
from jax.experimental import pallas as pl
from jax.experimental.pallas import tpu as pltpu
from jax.sharding import PartitionSpec as P

KX = 32
KY = 32
KZ = 8


tanh_coef = 0.7978845608028654
cubic_coef = 0.044715


def frequencies(kept_count, length):
    indices = jnp.arange(kept_count, dtype=jnp.int32)
    return jnp.where(indices < kept_count // 2, indices, indices + (length - kept_count))


def plane_table(count_y, count_z, kept_y, kept_z):
    freq_y = frequencies(kept_y, count_y)
    freq_z = jnp.arange(kept_z, dtype=jnp.int32)
    turn_y = jnp.arange(count_y, dtype=jnp.int32)[:, None] * freq_y[None, :] % count_y
    turn_z = jnp.arange(count_z, dtype=jnp.int32)[:, None] * freq_z[None, :] % count_z
    angles = (
        2.0
        * math.pi
        * (
            turn_y[:, None, :, None].astype(jnp.float32) / count_y
            + turn_z[None, :, None, :].astype(jnp.float32) / count_z
        )
    )
    factor = 1.0 / math.sqrt(count_y * count_z)
    basis_table = jnp.stack([factor * jnp.cos(angles), -factor * jnp.sin(angles)], axis=-1)
    return basis_table.reshape(count_y * count_z, kept_y * kept_z, 2).astype(jnp.bfloat16)


def line_table(full_length, kept_count):
    freq_x = frequencies(kept_count, full_length)
    turns = jnp.arange(full_length, dtype=jnp.int32)[:, None] * freq_x[None, :] % full_length
    angles = 2.0 * math.pi * turns.astype(jnp.float32) / full_length
    factor = 1.0 / math.sqrt(full_length)
    cos_part = factor * jnp.cos(angles)
    sine_part = factor * jnp.sin(angles)
    first_row = jnp.stack([cos_part, -sine_part], axis=1)
    second = jnp.stack([sine_part, cos_part], axis=1)
    return jnp.stack([first_row, second], axis=0).astype(jnp.bfloat16)


def mode_doubling(kept_y, kept_z):
    mode_index = jnp.arange(kept_y * kept_z, dtype=jnp.int32) % kept_z
    return jnp.where(mode_index == 0, 1.0, 2.0).astype(jnp.float32)


def gelu_slope(values):
    inner_arg = tanh_coef * (values + cubic_coef * values * values * values)
    tanh_part = jnp.tanh(inner_arg)
    return 0.5 * (1.0 + tanh_part) + 0.5 * values * (1.0 - tanh_part * tanh_part) * tanh_coef * (
        1.0 + 3.0 * cubic_coef * values * values
    )


def product(equation, left_op, right_op):
    return jnp.einsum(equation, left_op, right_op, preferred_element_type=jnp.float32)


def forward_lines(coarse, line_basis):
    return product("xpscm,pxqk->kqscm", coarse, line_basis).astype(jnp.bfloat16)


def inverse_lines(spectrum, line_basis):
    return product("kqscm,pxqk->xpscm", spectrum, line_basis).astype(jnp.bfloat16)


def spectral_mix(spectrum, weights):
    real_part = spectrum[:, 0]
    imag_part = spectrum[:, 1]
    w_real = weights[:, :, 0]
    w_imag = weights[:, :, 1]
    out_real = product("ksim,mkio->ksom", real_part, w_real) - product(
        "ksim,mkio->ksom", imag_part, w_imag
    )
    out_imag = product("ksim,mkio->ksom", real_part, w_imag) + product(
        "ksim,mkio->ksom", imag_part, w_real
    )
    return jnp.stack([out_real, out_imag], axis=1).astype(jnp.bfloat16)


def spectral_pull(adjoint, weights):
    real_part = adjoint[:, 0]
    imag_part = adjoint[:, 1]
    w_real = weights[:, :, 0]
    w_imag = weights[:, :, 1]
    out_real = product("ksom,mkio->ksim", real_part, w_real) + product(
        "ksom,mkio->ksim", imag_part, w_imag
    )
    out_imag = product("ksom,mkio->ksim", imag_part, w_real) - product(
        "ksom,mkio->ksim", real_part, w_imag
    )
    return jnp.stack([out_real, out_imag], axis=1).astype(jnp.bfloat16)


def weight_grad(spectrum, adjoint):
    spec_real = spectrum[:, 0]
    spec_imag = spectrum[:, 1]
    adj_real = adjoint[:, 0]
    adj_imag = adjoint[:, 1]
    grad_real = product("ksim,ksom->mkio", spec_real, adj_real) + product(
        "ksim,ksom->mkio", spec_imag, adj_imag
    )
    grad_imag = product("ksim,ksom->mkio", spec_real, adj_imag) - product(
        "ksim,ksom->mkio", spec_imag, adj_real
    )
    return jnp.stack([grad_real, grad_imag], axis=2)


def to_modes(coarse):
    return lax.all_to_all(coarse, "space", split_axis=4, concat_axis=0, tiled=True)


def to_cells(returned):
    return lax.all_to_all(returned, "space", split_axis=0, concat_axis=4, tiled=True)


def plain_body(features, cotangent, spectral, pointwise, biases):
    samples, channels, slab_cells, span_y, span_z = features.shape
    full_length = slab_cells * lax.axis_size("space")
    plane_basis = plane_table(span_y, span_z, KY, KZ)
    line_basis = line_table(full_length, KX)
    doubling = mode_doubling(KY, KZ)
    doubling_cells = doubling.astype(jnp.bfloat16)[None, None, None, None, :]
    flat_cells = features.reshape(samples, channels, slab_cells, span_y * span_z)
    coarse = product("scxq,qmp->xpscm", flat_cells, plane_basis).astype(jnp.bfloat16)
    spectrum = forward_lines(to_modes(coarse), line_basis)
    local_modes = spectral.shape[0]
    blocks = lax.all_gather(spectral, "dp", axis=1, tiled=True)
    weights = blocks.reshape(local_modes, blocks.shape[1], 2, channels, channels)
    mixed_modes = spectral_mix(spectrum, weights)
    returned = to_cells(inverse_lines(mixed_modes, line_basis))
    spectral_part = product("xpscm,qmp->scxq", returned * doubling_cells, plane_basis)
    linear = product("sicq,io->socq", flat_cells, pointwise)
    pre_act = linear + biases.astype(jnp.float32)[None, :, None, None] + spectral_part
    upstream_grad = cotangent.reshape(flat_cells.shape).astype(jnp.float32)
    delta_cells = (upstream_grad * gelu_slope(pre_act)).astype(jnp.bfloat16)
    coarse_back = (
        product("scxq,qmp->xpscm", delta_cells, plane_basis) * doubling[None, None, None, None, :]
    ).astype(jnp.bfloat16)
    adjoint = forward_lines(to_modes(coarse_back), line_basis)
    pulled = spectral_pull(adjoint, weights)
    grad_terms = weight_grad(spectrum, adjoint)
    grad_spectral = lax.psum_scatter(
        grad_terms.reshape(local_modes, KX, 2 * channels * channels).astype(jnp.bfloat16),
        "dp",
        scatter_dimension=1,
        tiled=True,
    ).astype(jnp.float32)
    back_cells = to_cells(inverse_lines(pulled, line_basis))
    grad_cells = product("socq,io->sicq", delta_cells, pointwise) + product(
        "xpscm,qmp->scxq", back_cells, plane_basis
    )
    grad_input = grad_cells.astype(jnp.bfloat16).reshape(features.shape)
    return (grad_input, grad_spectral)


HALVES = 2


def np_frequencies(kept_count, length):
    indices = np.arange(kept_count)
    return np.where(indices < kept_count // 2, indices, indices + (length - kept_count))


def np_plane_rows(count_y, count_z, blocks, tiles, quads):
    turn_y = np.arange(count_y)[:, None] * np_frequencies(KY, count_y)[None, :] % count_y
    turn_z = np.arange(count_z)[:, None] * np.arange(KZ)[None, :] % count_z
    angles = 2.0 * np.pi * (
        turn_y[:, None, :, None] / count_y + turn_z[None, :, None, :] / count_z
    )
    factor = 1.0 / math.sqrt(count_y * count_z)
    table = np.stack([factor * np.cos(angles), -factor * np.sin(angles)], axis=0)
    near = tiles // HALVES
    table = table.reshape(2, count_y * count_z, blocks, HALVES, near, quads)
    rows = table.transpose(5, 2, 3, 0, 4, 1).reshape(-1, count_y * count_z)
    doubling = np.where(np.arange(KY * KZ) % KZ == 0, 1.0, 2.0)
    doubling = doubling.reshape(blocks, HALVES, 1, near, quads)
    doubling = np.broadcast_to(doubling, (blocks, HALVES, 2, near, quads)).transpose(4, 0, 1, 2, 3)
    return rows.astype(ml_dtypes.bfloat16), doubling.reshape(-1, 1).astype(np.float32)


def np_line(full_length, blocks, owners):
    turns = np.arange(full_length)[:, None] * np_frequencies(KX, full_length)[None, :] % full_length
    angles = 2.0 * np.pi * turns / full_length
    factor = 1.0 / math.sqrt(full_length)
    cos_part, sine_part = factor * np.cos(angles), factor * np.sin(angles)
    table = np.stack(
        [np.stack([cos_part, -sine_part], 0), np.stack([sine_part, cos_part], 0)], 0
    )
    table = table.reshape(2, 2, blocks, full_length // blocks, owners, KX // owners)
    table = table.transpose(4, 1, 5, 2, 3, 0).reshape(2 * KX, 2 * full_length)
    return table.astype(ml_dtypes.bfloat16)


def np_selectors(channels, slab, quads):
    def one_hot(rows, columns, count_rows, count_columns):
        table = np.zeros((count_rows, count_columns), ml_dtypes.bfloat16)
        table[rows.reshape(-1), columns.reshape(-1)] = 1
        return table

    lanes = quads * channels
    j, c, x = np.meshgrid(np.arange(quads), np.arange(channels), np.arange(slab), indexing="ij")
    regroup = one_hot(
        (j * channels + c) * slab + x, (x * quads + j) * channels + c, lanes * slab, lanes * slab
    )
    j, i, o = np.meshgrid(
        np.arange(quads), np.arange(channels), np.arange(channels), indexing="ij"
    )
    spread = one_hot(
        j * channels + i,
        j * channels * channels + i * channels + o,
        lanes,
        quads * channels * channels,
    )
    spread = spread.reshape(lanes, quads, channels * channels).transpose(1, 0, 2)
    j, i, o = np.meshgrid(np.arange(quads), np.arange(quads), np.arange(channels), indexing="ij")
    tile = one_hot((j * quads + i) * channels + o, j * channels + o, quads * lanes, lanes)
    cells = np.arange(channels * slab)
    repeat = one_hot(cells, cells // slab, channels * slab, channels)
    flat = np.ascontiguousarray
    return regroup, flat(spread), flat(spread.transpose(0, 2, 1)), tile, flat(tile.T), repeat


f32, bf16 = jnp.float32, jnp.bfloat16
NT = (((1,), (1,)), ((), ()))
TN = (((0,), (0,)), ((), ()))


def dot(left, right):
    return jnp.dot(left, right, preferred_element_type=f32)


def dot_nt(left, right):
    return lax.dot_general(left, right, NT, preferred_element_type=f32)


def start_exchange(axis, count, send, recv, send_sem, recv_sem):
    me = lax.axis_index(axis)
    copies = []
    for step in range(1, count):
        peer = lax.rem(me + step, count)
        copy = pltpu.make_async_remote_copy(
            src_ref=send.at[peer],
            dst_ref=recv.at[me],
            send_sem=send_sem.at[step],
            recv_sem=recv_sem.at[step],
            device_id={axis: peer},
            device_id_type=pl.DeviceIdType.MESH,
        )
        copy.start()
        copies.append(copy)
    recv[me] = send[me]
    return copies


def wait_all(copies):
    for copy in copies:
        copy.wait()


def layer_kernel(
    sizes,
    feats, cot_hbm, weights_hbm, pointwise, biases, analysis_hbm, synthesis_hbm,
    regroup_hbm, spread_hbm, gather_hbm, tile_hbm, untile_hbm, repeat, doubling, line,
    out_cells, out_delta, out_grads, mix_back,
    cot, weights, analysis, synthesis, regroup, spread, gather, tile, untile, grads,
    natural, rows_in, delta, coarse_acc, volume, mix_fwd, bias,
    stack, parts, spec_wide, adj_wide, products, pulled, cells,
    space_send, space_recv, dp_send, dp_recv,
    load_sem, analysis_sem, space_ssem, space_rsem, dp_ssem, dp_rsem,
):
    blocks, owners, channels, slab, span_y, tiles, quads, kept = sizes
    lanes = quads * channels
    rows = 2 * kept * owners
    cell_rows = channels * slab
    width = feats.shape[1]
    cells_count = span_y * width
    chunk = analysis_hbm.shape[0] // analysis_sem.shape[0]
    chunks = cells_count // chunk
    lines = chunk // width
    group = blocks * 2 * tiles
    near = tiles // HALVES
    square = channels * channels
    mesh_id = pl.DeviceIdType.MESH

    analysis_loads = [
        pltpu.make_async_copy(
            analysis_hbm.at[pl.ds(step * chunk, chunk)],
            analysis.at[pl.ds(step * chunk, chunk)],
            analysis_sem.at[step],
        )
        for step in range(chunks)
    ]
    for copy in analysis_loads:
        copy.start()
    load_cot = pltpu.make_async_copy(cot_hbm, cot, load_sem.at[0])
    load_weights = pltpu.make_async_copy(weights_hbm, weights, load_sem.at[1])
    load_synthesis = pltpu.make_async_copy(synthesis_hbm, synthesis, load_sem.at[2])
    load_tables = [
        pltpu.make_async_copy(source, target, load_sem.at[5 + at])
        for at, (source, target) in enumerate(
            [(regroup_hbm, regroup), (spread_hbm, spread), (tile_hbm, tile),
             (untile_hbm, untile), (gather_hbm, gather)]
        )
    ]
    load_tables[0].start()
    load_cot.start()
    load_weights.start()
    for copy in load_tables[1:]:
        copy.start()
    load_synthesis.start()

    barrier = pltpu.get_barrier_semaphore()
    for axis, count in (("space", blocks), ("dp", owners)):
        me = lax.axis_index(axis)
        for step in range(1, count):
            pl.semaphore_signal(
                barrier, inc=1, device_id={axis: lax.rem(me + step, count)}, device_id_type=mesh_id
            )

    def widen(source):
        def some(step, _):
            at = pl.ds(pl.multiple_of(step * 512, 512), 512)
            natural[at, :] = source[at, :].astype(f32)
            return 0

        lax.fori_loop(0, natural.shape[0] // 512, some, 0)

    def plane_lines(step):
        return jnp.concatenate(
            [natural[pl.ds(step * lines + u, cell_rows, stride=span_y), :] for u in range(lines)],
            axis=1,
        )

    def columns(step):
        return pl.ds(pl.multiple_of(step * chunk, chunk), chunk)

    def send_space(turn, half):
        at = turn * HALVES + half
        return start_exchange(
            "space", blocks, space_send.at[at], space_recv.at[at],
            space_ssem.at[at], space_rsem.at[at],
        )

    def send_dp(turn, half):
        at = turn * HALVES + half
        return start_exchange(
            "dp", owners, dp_send.at[at], dp_recv.at[at], dp_ssem.at[at], dp_rsem.at[at]
        )

    def send_cells(turn, coarse):
        wide = jnp.concatenate(
            [coarse[:, j * group : (j + 1) * group].T.astype(bf16) for j in range(quads)], axis=1
        )
        wide = dot(wide, regroup[...])
        copies = []
        for half in range(HALVES):
            for block in range(blocks):
                at = (block * HALVES + half) * 2 * near
                pieces = [
                    wide[at : at + 2 * near, x * lanes : (x + 1) * lanes] for x in range(slab)
                ]
                space_send[turn * HALVES + half, block] = jnp.concatenate(pieces, axis=0).astype(
                    bf16
                )
            copies.append(send_space(turn, half))
        return copies

    def cells_to_modes(turn, dp_turn, arriving):
        copies = []
        for half in range(HALVES):
            wait_all(arriving[half])
            cells[half] = space_recv[turn * HALVES + half].astype(f32).reshape(cells.shape[1:])
            wide = jnp.concatenate(
                [cells[half, pl.ds(t, blocks * 2 * slab, stride=near), :] for t in range(near)],
                axis=1,
            ).astype(bf16)
            spectrum = dot(line[...], wide).astype(bf16)
            dp_send[dp_turn * HALVES + half] = spectrum.reshape(owners, 2 * kept, near * lanes)
            copies.append(send_dp(dp_turn, half))
        return copies

    def modes_to_cells(dp_turn, turn, arriving):
        copies = []
        for half in range(HALVES):
            wait_all(arriving[half])
            wide = dp_recv[dp_turn * HALVES + half].reshape(rows, near * lanes)
            back = lax.dot_general(line[...], wide, TN, preferred_element_type=f32)
            for t in range(near):
                cells[half, pl.ds(t, blocks * 2 * slab, stride=near), :] = back[
                    :, t * lanes : (t + 1) * lanes
                ]
            space_send[turn * HALVES + half] = (
                cells[half].astype(bf16).reshape(space_send.shape[1:])
            )
            copies.append(send_space(turn, half))
        return copies

    def stack_half(dp_turn, half):
        for t in range(near):
            stack[t * rows : (t + 1) * rows] = dp_recv[
                dp_turn * HALVES + half, :, :, t * lanes : (t + 1) * lanes
            ].reshape(rows, lanes)

    def unstack_half(dp_turn, half, values):
        for t in range(near):
            dp_send[dp_turn * HALVES + half, :, :, t * lanes : (t + 1) * lanes] = (
                values[t * rows : (t + 1) * rows].astype(bf16).reshape(owners, 2 * kept, lanes)
            )
        return send_dp(dp_turn, half)

    def weight_tiles(m, s):
        lo = s * 128
        return (
            weights[m, :, lo : lo + 128].astype(f32),
            weights[m, :, square + lo : square + lo + 128].astype(f32),
        )

    widen(feats)
    coarse_acc[...] = jnp.zeros_like(coarse_acc)
    for step in range(chunks):
        analysis_loads[step].wait()
        part = plane_lines(step).astype(bf16)
        rows_in[:, step * chunk : (step + 1) * chunk] = part
        coarse_acc[...] += dot(part, analysis[step * chunk : (step + 1) * chunk, :])
    pl.semaphore_wait(barrier, blocks + owners - 2)
    load_tables[0].wait()
    copies = send_cells(0, coarse_acc[...])

    same_cell = lax.rem(lax.broadcasted_iota(jnp.int32, mix_fwd.shape, 0), slab) == lax.rem(
        lax.broadcasted_iota(jnp.int32, mix_fwd.shape, 1), slab
    )
    spread_out = dot_nt(dot_nt(repeat[...], pointwise[...]).astype(bf16), repeat[...])
    mix_fwd[...] = jnp.where(same_cell, spread_out, 0.0).astype(bf16)
    spread_out = dot_nt(dot(repeat[...], pointwise[...]).astype(bf16), repeat[...])
    mix_back[...] = jnp.where(same_cell, spread_out, 0.0).astype(bf16)
    bias[...] = jnp.sum(
        repeat[...].astype(f32) * biases[...].astype(f32), axis=1, keepdims=True
    )
    load_cot.wait()
    widen(cot)
    copies = cells_to_modes(0, 0, copies)
    load_weights.wait()
    for copy in load_tables[1:]:
        copy.wait()

    back_copies = []
    for half in range(HALVES):
        wait_all(copies[half])
        stack_half(0, half)

        def mix(j, _, half=half):
            spec_wide[half, j] = dot(stack[...], spread[j])
            for t in range(near):
                m = (half * near + t) * quads + j
                base = t * rows
                total = [None] * (2 * owners)
                for s in range(square // 128):
                    lo = s * 128
                    w_re, w_im = weight_tiles(m, s)
                    for n in range(owners):
                        at = base + 2 * n * kept
                        re = spec_wide[half, j, at : at + kept, lo : lo + 128]
                        im = spec_wide[half, j, at + kept : at + 2 * kept, lo : lo + 128]
                        out_re = re * w_re - im * w_im
                        out_im = re * w_im + im * w_re
                        total[2 * n] = out_re if s == 0 else total[2 * n] + out_re
                        total[2 * n + 1] = out_im if s == 0 else total[2 * n + 1] + out_im
                parts[j, base : base + rows, :] = jnp.concatenate(total, axis=0).astype(bf16)
            return 0

        lax.fori_loop(0, quads, mix, 0)
        mixed = dot(jnp.concatenate([parts[j] for j in range(quads)], axis=1), tile[...])
        back_copies.append(unstack_half(1, half, mixed))
    copies = modes_to_cells(1, 1, back_copies)
    load_synthesis.wait()
    for half in range(HALVES):
        wait_all(copies[half])
    collect_volume(
        slab, space_recv.at[pl.ds(HALVES, HALVES)], regroup, volume, doubling
    )

    coarse_acc[...] = jnp.zeros_like(coarse_acc)

    def activate(step, _):
        at = columns(step)
        pre_act = dot(volume[...], synthesis[:, at]) + dot(mix_fwd[...], rows_in[:, at]) + bias[...]
        part = (plane_lines(step) * gelu_slope(pre_act)).astype(bf16)
        delta[:, at] = part
        coarse_acc[...] += dot(part, analysis[at, :])
        return 0

    lax.fori_loop(0, chunks, activate, 0)
    copies = send_cells(2, coarse_acc[...] * doubling[...])
    store_delta = pltpu.make_async_copy(delta, out_delta, load_sem.at[4])
    store_delta.start()
    copies = cells_to_modes(2, 2, copies)

    back_copies = []
    for half in range(HALVES):
        wait_all(copies[half])
        stack_half(2, half)
        wide = dot(stack[...], untile[...])
        for j in range(quads):
            adj_wide[half, j] = wide[:, j * lanes : (j + 1) * lanes]
        pulled[...] = jnp.zeros_like(pulled)

        def pull(j, _, half=half):
            for t in range(near):
                m = (half * near + t) * quads + j
                base = t * rows
                adjs = [
                    adj_wide[half, j, base + r * kept : base + (r + 1) * kept]
                    for r in range(2 * owners)
                ]
                for s in range(square // 128):
                    w_re, w_im = weight_tiles(m, s)
                    terms = []
                    for n in range(owners):
                        re, im = adjs[2 * n], adjs[2 * n + 1]
                        terms += [re * w_re + im * w_im, im * w_re - re * w_im]
                    products[base : base + rows, s * 128 : (s + 1) * 128] = jnp.concatenate(
                        terms, axis=0
                    ).astype(bf16)
            pulled[...] += dot(products[...], gather[j])
            return 0

        lax.fori_loop(0, quads, pull, 0)
        back_copies.append(unstack_half(3, half, pulled[...]))

    for half in range(HALVES):

        def weight_terms(j, _, half=half):
            for t in range(near):
                m = (half * near + t) * quads + j
                base = t * rows
                adjs = [
                    adj_wide[half, j, base + r * kept : base + (r + 1) * kept]
                    for r in range(2 * owners)
                ]
                for s in range(square // 128):
                    lo = s * 128
                    grad_re, grad_im = None, None
                    for n in range(owners):
                        at = base + 2 * n * kept
                        re = spec_wide[half, j, at : at + kept, lo : lo + 128]
                        im = spec_wide[half, j, at + kept : at + 2 * kept, lo : lo + 128]
                        a_re, a_im = adjs[2 * n], adjs[2 * n + 1]
                        term_re = re * a_re + im * a_im
                        term_im = re * a_im - im * a_re
                        grad_re = term_re if n == 0 else grad_re + term_re
                        grad_im = term_im if n == 0 else grad_im + term_im
                    grads[m, :, lo : lo + 128] = grad_re
                    grads[m, :, square + lo : square + lo + 128] = grad_im
            return 0

        lax.fori_loop(0, quads, weight_terms, 0)
    store_grads = pltpu.make_async_copy(grads, out_grads, load_sem.at[3])
    store_grads.start()
    copies = modes_to_cells(3, 3, back_copies)
    for half in range(HALVES):
        wait_all(copies[half])
        out_cells[half] = space_recv[3 * HALVES + half]
    store_delta.wait()
    store_grads.wait()


def collect_volume(slab, arrived, regroup, volume, doubling):
    pieces = []
    lanes = arrived.shape[3]
    tile_rows = arrived.shape[2] // slab
    group = arrived.shape[1] * HALVES * tile_rows
    for block in range(arrived.shape[1]):
        for half in range(HALVES):
            held = arrived[half, block].astype(f32)
            pieces.append(
                jnp.concatenate(
                    [held[x * tile_rows : (x + 1) * tile_rows] for x in range(slab)], axis=1
                )
            )
    wide = dot_nt(jnp.concatenate(pieces, axis=0).astype(bf16), regroup[...])
    for j in range(wide.shape[1] // lanes):
        part = wide[:, j * lanes : (j + 1) * lanes].T
        if doubling is not None:
            part = part * doubling[:, j * group : (j + 1) * group]
        volume[:, j * group : (j + 1) * group] = part.astype(bf16)


def result_kernel(
    slab, arrived, mix_back, regroup, delta_hbm, grads_hbm, synthesis_hbm,
    out_input, out_spectral,
    delta, synthesis, volume, natural, sems, synthesis_sem,
):
    cell_rows, cells_count = delta.shape
    chunks = synthesis_sem.shape[0]
    chunk = cells_count // chunks
    width = natural.shape[1]
    lines = chunk // width
    span_y = cells_count // width
    load_delta = pltpu.make_async_copy(delta_hbm, delta, sems.at[0])
    load_delta.start()
    loads = [
        pltpu.make_async_copy(
            synthesis_hbm.at[:, pl.ds(step * chunk, chunk)],
            synthesis.at[:, pl.ds(step * chunk, chunk)],
            synthesis_sem.at[step],
        )
        for step in range(chunks)
    ]
    for copy in loads:
        copy.start()
    pass_grads = pltpu.make_async_copy(grads_hbm, out_spectral, sems.at[1])
    pass_grads.start()
    collect_volume(slab, arrived, regroup, volume, None)
    load_delta.wait()
    for step in range(chunks):
        loads[step].wait()
        at = slice(step * chunk, (step + 1) * chunk)
        grad = dot(volume[...], synthesis[:, at]) + dot(mix_back[...], delta[:, at])
        for u in range(lines):
            natural[pl.ds(step * lines + u, cell_rows, stride=span_y), :] = grad[
                :, u * width : (u + 1) * width
            ]

    def narrow(step, _):
        at = pl.ds(pl.multiple_of(step * 512, 512), 512)
        out_input[at, :] = natural[at, :].astype(bf16)
        return 0

    lax.fori_loop(0, natural.shape[0] // 512, narrow, 0)
    pass_grads.wait()


def fits(features, spectral, owners):
    samples, channels, slab, span_y, span_z = features.shape
    modes, kept = spectral.shape[:2]
    return (
        samples == 1 and kept == 8 and channels == 32 and slab == 4 and modes == 32
        and span_z == 128 and span_y % 8 == 0 and (2 * kept * owners) % 16 == 0
    )


def body(features, cotangent, spectral, pointwise, biases):
    blocks, owners = lax.axis_size("space"), lax.axis_size("dp")
    if not fits(features, spectral, owners):
        return plain_body(features, cotangent, spectral, pointwise, biases)
    _, channels, slab, span_y, span_z = features.shape
    modes, kept = spectral.shape[:2]
    tiles = 8
    quads = modes // tiles
    lanes = quads * channels
    square = channels * channels
    cell_rows, cells_count = channels * slab, span_y * span_z
    natural_shape = (cell_rows * span_y, span_z)
    plane, doubling = np_plane_rows(span_y, span_z, blocks, tiles, quads)
    line = np_line(slab * blocks, blocks, owners)
    plane_rows = plane.shape[0]
    chunks = 8
    rows = 2 * kept * owners
    half_rows = rows * tiles // HALVES
    sizes = (blocks, owners, channels, slab, span_y, tiles, quads, kept)
    vmem = pl.BlockSpec(memory_space=pltpu.VMEM)
    hbm = pl.BlockSpec(memory_space=pl.ANY)
    space_shape = (4 * HALVES, blocks, 2 * slab * tiles // HALVES, lanes)
    dp_shape = (4 * HALVES, owners, 2 * kept, tiles // HALVES * lanes)
    regroup, spread, gather, tile, untile, repeat = np_selectors(channels, slab, quads)
    arrived, delta, grads, mix_back = pl.pallas_call(
        functools.partial(layer_kernel, sizes),
        out_shape=(
            jax.ShapeDtypeStruct((HALVES,) + space_shape[1:], bf16),
            jax.ShapeDtypeStruct((cell_rows, cells_count), bf16),
            jax.ShapeDtypeStruct(spectral.shape, f32),
            jax.ShapeDtypeStruct((cell_rows, cell_rows), bf16),
        ),
        in_specs=[vmem, hbm, hbm, vmem, vmem] + [hbm] * 7 + [vmem] * 3,
        out_specs=(vmem, hbm, hbm, vmem),
        scratch_shapes=[
            pltpu.VMEM(natural_shape, bf16),
            pltpu.VMEM(spectral.shape, bf16),
            pltpu.VMEM((cells_count, plane_rows), bf16),
            pltpu.VMEM((plane_rows, cells_count), bf16),
            pltpu.VMEM(regroup.shape, bf16),
            pltpu.VMEM(spread.shape, bf16),
            pltpu.VMEM(gather.shape, bf16),
            pltpu.VMEM(tile.shape, bf16),
            pltpu.VMEM(untile.shape, bf16),
            pltpu.VMEM(spectral.shape, f32),
            pltpu.VMEM(natural_shape, f32),
            pltpu.VMEM((cell_rows, cells_count), bf16),
            pltpu.VMEM((cell_rows, cells_count), bf16),
            pltpu.VMEM((cell_rows, plane_rows), f32),
            pltpu.VMEM((cell_rows, plane_rows), bf16),
            pltpu.VMEM((cell_rows, cell_rows), bf16),
            pltpu.VMEM((cell_rows, 1), f32),
            pltpu.VMEM((half_rows, lanes), bf16),
            pltpu.VMEM((quads, half_rows, lanes), bf16),
            pltpu.VMEM((HALVES, quads, half_rows, square), f32),
            pltpu.VMEM((HALVES, quads, half_rows, lanes), f32),
            pltpu.VMEM((half_rows, square), bf16),
            pltpu.VMEM((half_rows, lanes), f32),
            pltpu.VMEM((HALVES, blocks * 2 * slab * tiles // HALVES, lanes), f32),
            pltpu.VMEM(space_shape, bf16),
            pltpu.VMEM(space_shape, bf16),
            pltpu.VMEM(dp_shape, bf16),
            pltpu.VMEM(dp_shape, bf16),
            pltpu.SemaphoreType.DMA((10,)),
            pltpu.SemaphoreType.DMA((chunks,)),
            pltpu.SemaphoreType.DMA((4 * HALVES, blocks)),
            pltpu.SemaphoreType.DMA((4 * HALVES, blocks)),
            pltpu.SemaphoreType.DMA((4 * HALVES, owners)),
            pltpu.SemaphoreType.DMA((4 * HALVES, owners)),
        ],
        compiler_params=pltpu.CompilerParams(
            collective_id=0, has_side_effects=True, vmem_limit_bytes=56 * 1024 * 1024
        ),
    )(
        features.reshape(natural_shape),
        cotangent.reshape(natural_shape),
        spectral, pointwise, biases[None, :],
        np.ascontiguousarray(plane.T), plane,
        regroup, spread, gather, tile, untile, repeat, doubling.T, line,
    )
    grad_input, grad_spectral = pl.pallas_call(
        functools.partial(result_kernel, slab),
        out_shape=(
            jax.ShapeDtypeStruct(natural_shape, bf16),
            jax.ShapeDtypeStruct(spectral.shape, f32),
        ),
        in_specs=[vmem, vmem, vmem, hbm, hbm, hbm],
        out_specs=(vmem, hbm),
        scratch_shapes=[
            pltpu.VMEM((cell_rows, cells_count), bf16),
            pltpu.VMEM((plane_rows, cells_count), bf16),
            pltpu.VMEM((cell_rows, plane_rows), bf16),
            pltpu.VMEM(natural_shape, f32),
            pltpu.SemaphoreType.DMA((2,)),
            pltpu.SemaphoreType.DMA((chunks,)),
        ],
        compiler_params=pltpu.CompilerParams(vmem_limit_bytes=56 * 1024 * 1024),
    )(arrived, mix_back, regroup, delta, grads, plane)
    return grad_input.reshape(features.shape), grad_spectral


def solution(mesh):
    placed = (
        P("dp", None, "space", None, None),
        P("dp", None, "space", None, None),
        P("space", "dp", None),
        P(),
        P(),
    )
    return jax.shard_map(
        body,
        mesh=mesh,
        in_specs=placed,
        out_specs=(P("dp", None, "space", None, None), P("space", "dp", None)),
        check_vma=False,
    )
```

```python
import functools
import math

import jax
import jax.numpy as jnp
import ml_dtypes
import numpy as np
from jax import lax
from jax.experimental import pallas as pl
from jax.experimental.pallas import tpu as pltpu
from jax.sharding import PartitionSpec as P

KX = 32
KY = 32
KZ = 8


tanh_coef = 0.7978845608028654
cubic_coef = 0.044715


def frequencies(kept_count, length):
    indices = jnp.arange(kept_count, dtype=jnp.int32)
    return jnp.where(indices < kept_count // 2, indices, indices + (length - kept_count))


def plane_table(count_y, count_z, kept_y, kept_z):
    freq_y = frequencies(kept_y, count_y)
    freq_z = jnp.arange(kept_z, dtype=jnp.int32)
    turn_y = jnp.arange(count_y, dtype=jnp.int32)[:, None] * freq_y[None, :] % count_y
    turn_z = jnp.arange(count_z, dtype=jnp.int32)[:, None] * freq_z[None, :] % count_z
    angles = (
        2.0
        * math.pi
        * (
            turn_y[:, None, :, None].astype(jnp.float32) / count_y
            + turn_z[None, :, None, :].astype(jnp.float32) / count_z
        )
    )
    factor = 1.0 / math.sqrt(count_y * count_z)
    basis_table = jnp.stack([factor * jnp.cos(angles), -factor * jnp.sin(angles)], axis=-1)
    return basis_table.reshape(count_y * count_z, kept_y * kept_z, 2).astype(jnp.bfloat16)


def line_table(full_length, kept_count):
    freq_x = frequencies(kept_count, full_length)
    turns = jnp.arange(full_length, dtype=jnp.int32)[:, None] * freq_x[None, :] % full_length
    angles = 2.0 * math.pi * turns.astype(jnp.float32) / full_length
    factor = 1.0 / math.sqrt(full_length)
    cos_part = factor * jnp.cos(angles)
    sine_part = factor * jnp.sin(angles)
    first_row = jnp.stack([cos_part, -sine_part], axis=1)
    second = jnp.stack([sine_part, cos_part], axis=1)
    return jnp.stack([first_row, second], axis=0).astype(jnp.bfloat16)


def mode_doubling(kept_y, kept_z):
    mode_index = jnp.arange(kept_y * kept_z, dtype=jnp.int32) % kept_z
    return jnp.where(mode_index == 0, 1.0, 2.0).astype(jnp.float32)


def gelu_slope(values):
    inner_arg = tanh_coef * (values + cubic_coef * values * values * values)
    tanh_part = jnp.tanh(inner_arg)
    return 0.5 * (1.0 + tanh_part) + 0.5 * values * (1.0 - tanh_part * tanh_part) * tanh_coef * (
        1.0 + 3.0 * cubic_coef * values * values
    )


def product(equation, left_op, right_op):
    return jnp.einsum(equation, left_op, right_op, preferred_element_type=jnp.float32)


def forward_lines(coarse, line_basis):
    return product("xpscm,pxqk->kqscm", coarse, line_basis).astype(jnp.bfloat16)


def inverse_lines(spectrum, line_basis):
    return product("kqscm,pxqk->xpscm", spectrum, line_basis).astype(jnp.bfloat16)


def spectral_mix(spectrum, weights):
    real_part = spectrum[:, 0]
    imag_part = spectrum[:, 1]
    w_real = weights[:, :, 0]
    w_imag = weights[:, :, 1]
    out_real = product("ksim,mkio->ksom", real_part, w_real) - product(
        "ksim,mkio->ksom", imag_part, w_imag
    )
    out_imag = product("ksim,mkio->ksom", real_part, w_imag) + product(
        "ksim,mkio->ksom", imag_part, w_real
    )
    return jnp.stack([out_real, out_imag], axis=1).astype(jnp.bfloat16)


def spectral_pull(adjoint, weights):
    real_part = adjoint[:, 0]
    imag_part = adjoint[:, 1]
    w_real = weights[:, :, 0]
    w_imag = weights[:, :, 1]
    out_real = product("ksom,mkio->ksim", real_part, w_real) + product(
        "ksom,mkio->ksim", imag_part, w_imag
    )
    out_imag = product("ksom,mkio->ksim", imag_part, w_real) - product(
        "ksom,mkio->ksim", real_part, w_imag
    )
    return jnp.stack([out_real, out_imag], axis=1).astype(jnp.bfloat16)


def weight_grad(spectrum, adjoint):
    spec_real = spectrum[:, 0]
    spec_imag = spectrum[:, 1]
    adj_real = adjoint[:, 0]
    adj_imag = adjoint[:, 1]
    grad_real = product("ksim,ksom->mkio", spec_real, adj_real) + product(
        "ksim,ksom->mkio", spec_imag, adj_imag
    )
    grad_imag = product("ksim,ksom->mkio", spec_real, adj_imag) - product(
        "ksim,ksom->mkio", spec_imag, adj_real
    )
    return jnp.stack([grad_real, grad_imag], axis=2)


def to_modes(coarse):
    return lax.all_to_all(coarse, "space", split_axis=4, concat_axis=0, tiled=True)


def to_cells(returned):
    return lax.all_to_all(returned, "space", split_axis=0, concat_axis=4, tiled=True)


def plain_body(features, cotangent, spectral, pointwise, biases):
    samples, channels, slab_cells, span_y, span_z = features.shape
    full_length = slab_cells * lax.axis_size("space")
    plane_basis = plane_table(span_y, span_z, KY, KZ)
    line_basis = line_table(full_length, KX)
    doubling = mode_doubling(KY, KZ)
    doubling_cells = doubling.astype(jnp.bfloat16)[None, None, None, None, :]
    flat_cells = features.reshape(samples, channels, slab_cells, span_y * span_z)
    coarse = product("scxq,qmp->xpscm", flat_cells, plane_basis).astype(jnp.bfloat16)
    spectrum = forward_lines(to_modes(coarse), line_basis)
    local_modes = spectral.shape[0]
    blocks = lax.all_gather(spectral, "dp", axis=1, tiled=True)
    weights = blocks.reshape(local_modes, blocks.shape[1], 2, channels, channels)
    mixed_modes = spectral_mix(spectrum, weights)
    returned = to_cells(inverse_lines(mixed_modes, line_basis))
    spectral_part = product("xpscm,qmp->scxq", returned * doubling_cells, plane_basis)
    linear = product("sicq,io->socq", flat_cells, pointwise)
    pre_act = linear + biases.astype(jnp.float32)[None, :, None, None] + spectral_part
    upstream_grad = cotangent.reshape(flat_cells.shape).astype(jnp.float32)
    delta_cells = (upstream_grad * gelu_slope(pre_act)).astype(jnp.bfloat16)
    coarse_back = (
        product("scxq,qmp->xpscm", delta_cells, plane_basis) * doubling[None, None, None, None, :]
    ).astype(jnp.bfloat16)
    adjoint = forward_lines(to_modes(coarse_back), line_basis)
    pulled = spectral_pull(adjoint, weights)
    grad_terms = weight_grad(spectrum, adjoint)
    grad_spectral = lax.psum_scatter(
        grad_terms.reshape(local_modes, KX, 2 * channels * channels).astype(jnp.bfloat16),
        "dp",
        scatter_dimension=1,
        tiled=True,
    ).astype(jnp.float32)
    back_cells = to_cells(inverse_lines(pulled, line_basis))
    grad_cells = product("socq,io->sicq", delta_cells, pointwise) + product(
        "xpscm,qmp->scxq", back_cells, plane_basis
    )
    grad_input = grad_cells.astype(jnp.bfloat16).reshape(features.shape)
    return (grad_input, grad_spectral)


HALVES = 2


def np_frequencies(kept_count, length):
    indices = np.arange(kept_count)
    return np.where(indices < kept_count // 2, indices, indices + (length - kept_count))


def np_plane_rows(count_y, count_z, blocks, tiles, quads):
    turn_y = np.arange(count_y)[:, None] * np_frequencies(KY, count_y)[None, :] % count_y
    turn_z = np.arange(count_z)[:, None] * np.arange(KZ)[None, :] % count_z
    angles = 2.0 * np.pi * (
        turn_y[:, None, :, None] / count_y + turn_z[None, :, None, :] / count_z
    )
    factor = 1.0 / math.sqrt(count_y * count_z)
    table = np.stack([factor * np.cos(angles), -factor * np.sin(angles)], axis=0)
    near = tiles // HALVES
    table = table.reshape(2, count_y * count_z, blocks, HALVES, near, quads)
    rows = table.transpose(3, 5, 2, 0, 4, 1).reshape(-1, count_y * count_z)
    doubling = np.where(np.arange(KY * KZ) % KZ == 0, 1.0, 2.0)
    doubling = doubling.reshape(blocks, HALVES, 1, near, quads)
    doubling = np.broadcast_to(doubling, (blocks, HALVES, 2, near, quads)).transpose(1, 4, 0, 2, 3)
    return rows.astype(ml_dtypes.bfloat16), doubling.reshape(-1, 1).astype(np.float32)


def np_line(full_length, blocks, owners):
    turns = np.arange(full_length)[:, None] * np_frequencies(KX, full_length)[None, :] % full_length
    angles = 2.0 * np.pi * turns / full_length
    factor = 1.0 / math.sqrt(full_length)
    cos_part, sine_part = factor * np.cos(angles), factor * np.sin(angles)
    table = np.stack(
        [np.stack([cos_part, -sine_part], 0), np.stack([sine_part, cos_part], 0)], 0
    )
    table = table.reshape(2, 2, blocks, full_length // blocks, owners, KX // owners)
    table = table.transpose(4, 1, 5, 2, 3, 0).reshape(2 * KX, 2 * full_length)
    return table.astype(ml_dtypes.bfloat16)


def np_selectors(channels, slab, quads):
    def one_hot(rows, columns, count_rows, count_columns):
        table = np.zeros((count_rows, count_columns), ml_dtypes.bfloat16)
        table[rows.reshape(-1), columns.reshape(-1)] = 1
        return table

    lanes = quads * channels
    j, c, x = np.meshgrid(np.arange(quads), np.arange(channels), np.arange(slab), indexing="ij")
    regroup = one_hot(
        (j * channels + c) * slab + x, (x * quads + j) * channels + c, lanes * slab, lanes * slab
    )
    j, i, o = np.meshgrid(
        np.arange(quads), np.arange(channels), np.arange(channels), indexing="ij"
    )
    spread = one_hot(
        j * channels + i,
        j * channels * channels + i * channels + o,
        lanes,
        quads * channels * channels,
    )
    spread = spread.reshape(lanes, quads, channels * channels).transpose(1, 0, 2)
    j, i, o = np.meshgrid(np.arange(quads), np.arange(quads), np.arange(channels), indexing="ij")
    tile = one_hot((j * quads + i) * channels + o, j * channels + o, quads * lanes, lanes)
    cells = np.arange(channels * slab)
    repeat = one_hot(cells, cells // slab, channels * slab, channels)
    flat = np.ascontiguousarray
    return regroup, flat(spread), flat(spread.transpose(0, 2, 1)), tile, flat(tile.T), repeat


f32, bf16 = jnp.float32, jnp.bfloat16
NT = (((1,), (1,)), ((), ()))
TN = (((0,), (0,)), ((), ()))


def dot(left, right):
    return jnp.dot(left, right, preferred_element_type=f32)


def dot_nt(left, right):
    return lax.dot_general(left, right, NT, preferred_element_type=f32)


def start_exchange(axis, count, send, recv, send_sem, recv_sem):
    me = lax.axis_index(axis)
    copies = []
    for step in range(1, count):
        peer = lax.rem(me + step, count)
        copy = pltpu.make_async_remote_copy(
            src_ref=send.at[peer],
            dst_ref=recv.at[me],
            send_sem=send_sem.at[step],
            recv_sem=recv_sem.at[step],
            device_id={axis: peer},
            device_id_type=pl.DeviceIdType.MESH,
        )
        copy.start()
        copies.append(copy)
    recv[me] = send[me]
    return copies


def wait_all(copies):
    for copy in copies:
        copy.wait()


def layer_kernel(
    sizes,
    feats, cot_hbm, weights_hbm, pointwise, biases, analysis_hbm, synthesis_hbm,
    regroup_hbm, spread_hbm, gather_hbm, tile_hbm, untile_hbm, repeat, doubling, line,
    out_cells, out_delta, out_grads, mix_back,
    cot, weights, analysis, synthesis, regroup, spread, gather, tile, untile, grads,
    natural, rows_in, linear, upstream, delta, coarse_acc, volume, mix_fwd, bias,
    stack, parts, spec_wide, adj_wide, products, pulled, cells,
    space_send, space_recv, dp_send, dp_recv,
    load_sem, analysis_sem, space_ssem, space_rsem, dp_ssem, dp_rsem,
):
    blocks, owners, channels, slab, span_y, tiles, quads, kept = sizes
    lanes = quads * channels
    rows = 2 * kept * owners
    cell_rows = channels * slab
    width = feats.shape[1]
    cells_count = span_y * width
    chunk = analysis_hbm.shape[0] // analysis_sem.shape[0]
    chunks = cells_count // chunk
    lines = chunk // width
    near = tiles // HALVES
    group = blocks * 2 * near
    part_columns = quads * group
    square = channels * channels
    mesh_id = pl.DeviceIdType.MESH

    analysis_loads = [
        pltpu.make_async_copy(
            analysis_hbm.at[pl.ds(step * chunk, chunk)],
            analysis.at[pl.ds(step * chunk, chunk)],
            analysis_sem.at[step],
        )
        for step in range(chunks)
    ]
    for copy in analysis_loads:
        copy.start()
    load_cot = pltpu.make_async_copy(cot_hbm, cot, load_sem.at[0])
    load_weights = pltpu.make_async_copy(weights_hbm, weights, load_sem.at[1])
    load_synthesis = pltpu.make_async_copy(synthesis_hbm, synthesis, load_sem.at[2])
    load_tables = [
        pltpu.make_async_copy(source, target, load_sem.at[5 + at])
        for at, (source, target) in enumerate(
            [(regroup_hbm, regroup), (spread_hbm, spread), (tile_hbm, tile),
             (untile_hbm, untile), (gather_hbm, gather)]
        )
    ]
    load_tables[0].start()
    load_cot.start()
    load_weights.start()
    for copy in load_tables[1:]:
        copy.start()
    load_synthesis.start()

    barrier = pltpu.get_barrier_semaphore()
    for axis, count in (("space", blocks), ("dp", owners)):
        me = lax.axis_index(axis)
        for step in range(1, count):
            pl.semaphore_signal(
                barrier, inc=1, device_id={axis: lax.rem(me + step, count)}, device_id_type=mesh_id
            )

    def widen(source):
        def some(step, _):
            at = pl.ds(pl.multiple_of(step * 512, 512), 512)
            natural[at, :] = source[at, :].astype(f32)
            return 0

        lax.fori_loop(0, natural.shape[0] // 512, some, 0)

    def plane_lines(step):
        return jnp.concatenate(
            [natural[pl.ds(step * lines + u, cell_rows, stride=span_y), :] for u in range(lines)],
            axis=1,
        )

    def columns(step):
        return pl.ds(pl.multiple_of(step * chunk, chunk), chunk)

    def send_space(turn, half):
        at = turn * HALVES + half
        return start_exchange(
            "space", blocks, space_send.at[at], space_recv.at[at],
            space_ssem.at[at], space_rsem.at[at],
        )

    def send_dp(turn, half):
        at = turn * HALVES + half
        return start_exchange(
            "dp", owners, dp_send.at[at], dp_recv.at[at], dp_ssem.at[at], dp_rsem.at[at]
        )

    def send_cells(turn, half, coarse):
        wide = jnp.concatenate(
            [coarse[:, j * group : (j + 1) * group].T.astype(bf16) for j in range(quads)], axis=1
        )
        wide = dot(wide, regroup[...])
        for block in range(blocks):
            at = block * 2 * near
            pieces = [wide[at : at + 2 * near, x * lanes : (x + 1) * lanes] for x in range(slab)]
            space_send[turn * HALVES + half, block] = jnp.concatenate(pieces, axis=0).astype(bf16)
        return send_space(turn, half)

    def cells_to_modes(turn, dp_turn, arriving):
        copies = []
        for half in range(HALVES):
            wait_all(arriving[half])
            cells[half] = space_recv[turn * HALVES + half].astype(f32).reshape(cells.shape[1:])
            wide = jnp.concatenate(
                [cells[half, pl.ds(t, blocks * 2 * slab, stride=near), :] for t in range(near)],
                axis=1,
            ).astype(bf16)
            spectrum = dot(line[...], wide).astype(bf16)
            dp_send[dp_turn * HALVES + half] = spectrum.reshape(owners, 2 * kept, near * lanes)
            copies.append(send_dp(dp_turn, half))
        return copies

    def modes_to_cells(dp_turn, turn, arriving):
        copies = []
        for half in range(HALVES):
            wait_all(arriving[half])
            wide = dp_recv[dp_turn * HALVES + half].reshape(rows, near * lanes)
            back = lax.dot_general(line[...], wide, TN, preferred_element_type=f32)
            for t in range(near):
                cells[half, pl.ds(t, blocks * 2 * slab, stride=near), :] = back[
                    :, t * lanes : (t + 1) * lanes
                ]
            space_send[turn * HALVES + half] = (
                cells[half].astype(bf16).reshape(space_send.shape[1:])
            )
            copies.append(send_space(turn, half))
        return copies

    def stack_half(dp_turn, half):
        for t in range(near):
            stack[t * rows : (t + 1) * rows] = dp_recv[
                dp_turn * HALVES + half, :, :, t * lanes : (t + 1) * lanes
            ].reshape(rows, lanes)

    def unstack_half(dp_turn, half, values):
        for t in range(near):
            dp_send[dp_turn * HALVES + half, :, :, t * lanes : (t + 1) * lanes] = (
                values[t * rows : (t + 1) * rows].astype(bf16).reshape(owners, 2 * kept, lanes)
            )
        return send_dp(dp_turn, half)

    def weight_tiles(m, s):
        lo = s * 128
        return (
            weights[m, :, lo : lo + 128].astype(f32),
            weights[m, :, square + lo : square + lo + 128].astype(f32),
        )

    widen(feats)
    for step in range(chunks):
        rows_in[:, step * chunk : (step + 1) * chunk] = plane_lines(step).astype(bf16)

    def analyse(half, source):
        at = slice(half * part_columns, (half + 1) * part_columns)
        coarse_acc[...] = jnp.zeros_like(coarse_acc)
        for step in range(chunks):
            if half == 0 and source is rows_in:
                analysis_loads[step].wait()
            rows_at = slice(step * chunk, (step + 1) * chunk)
            coarse_acc[...] += dot(source[:, rows_at], analysis[rows_at, at])
        return coarse_acc[...]

    coarse = analyse(0, rows_in)
    pl.semaphore_wait(barrier, blocks + owners - 2)
    load_tables[0].wait()
    copies = [send_cells(0, 0, coarse)]
    for half in range(1, HALVES):
        copies.append(send_cells(0, half, analyse(half, rows_in)))

    same_cell = lax.rem(lax.broadcasted_iota(jnp.int32, mix_fwd.shape, 0), slab) == lax.rem(
        lax.broadcasted_iota(jnp.int32, mix_fwd.shape, 1), slab
    )
    spread_out = dot_nt(dot_nt(repeat[...], pointwise[...]).astype(bf16), repeat[...])
    mix_fwd[...] = jnp.where(same_cell, spread_out, 0.0).astype(bf16)
    spread_out = dot_nt(dot(repeat[...], pointwise[...]).astype(bf16), repeat[...])
    mix_back[...] = jnp.where(same_cell, spread_out, 0.0).astype(bf16)
    bias[...] = jnp.sum(
        repeat[...].astype(f32) * biases[...].astype(f32), axis=1, keepdims=True
    )
    load_cot.wait()
    widen(cot)

    def prepare(step, _):
        at = columns(step)
        linear[:, at] = dot(mix_fwd[...], rows_in[:, at]) + bias[...]
        upstream[:, at] = plane_lines(step)
        return 0

    lax.fori_loop(0, chunks, prepare, 0)
    copies = cells_to_modes(0, 0, copies)
    load_weights.wait()
    for copy in load_tables[1:]:
        copy.wait()

    back_copies = []
    for half in range(HALVES):
        wait_all(copies[half])
        stack_half(0, half)

        def mix(j, _, half=half):
            spec_wide[half, j] = dot(stack[...], spread[j])
            for t in range(near):
                m = (half * near + t) * quads + j
                base = t * rows
                total = [None] * (2 * owners)
                for s in range(square // 128):
                    lo = s * 128
                    w_re, w_im = weight_tiles(m, s)
                    for n in range(owners):
                        at = base + 2 * n * kept
                        re = spec_wide[half, j, at : at + kept, lo : lo + 128]
                        im = spec_wide[half, j, at + kept : at + 2 * kept, lo : lo + 128]
                        out_re = re * w_re - im * w_im
                        out_im = re * w_im + im * w_re
                        total[2 * n] = out_re if s == 0 else total[2 * n] + out_re
                        total[2 * n + 1] = out_im if s == 0 else total[2 * n + 1] + out_im
                parts[j, base : base + rows, :] = jnp.concatenate(total, axis=0).astype(bf16)
            return 0

        lax.fori_loop(0, quads, mix, 0)
        mixed = dot(jnp.concatenate([parts[j] for j in range(quads)], axis=1), tile[...])
        back_copies.append(unstack_half(1, half, mixed))
    copies = modes_to_cells(1, 1, back_copies)
    load_synthesis.wait()
    for half in range(HALVES):
        wait_all(copies[half])
        collect_volume(
            slab, half, space_recv.at[HALVES + half], regroup, volume, doubling
        )

    def activate(step, _):
        at = columns(step)
        pre_act = dot(volume[...], synthesis[:, at]) + linear[:, at]
        delta[:, at] = (upstream[:, at] * gelu_slope(pre_act)).astype(bf16)
        return 0

    lax.fori_loop(0, chunks, activate, 0)
    copies = []
    for half in range(HALVES):
        at = slice(half * part_columns, (half + 1) * part_columns)
        copies.append(send_cells(2, half, analyse(half, delta) * doubling[:, at]))
    store_delta = pltpu.make_async_copy(delta, out_delta, load_sem.at[4])
    store_delta.start()
    copies = cells_to_modes(2, 2, copies)

    back_copies = []
    for half in range(HALVES):
        wait_all(copies[half])
        stack_half(2, half)
        wide = dot(stack[...], untile[...])
        for j in range(quads):
            adj_wide[half, j] = wide[:, j * lanes : (j + 1) * lanes]
        pulled[...] = jnp.zeros_like(pulled)

        def pull(j, _, half=half):
            for t in range(near):
                m = (half * near + t) * quads + j
                base = t * rows
                adjs = [
                    adj_wide[half, j, base + r * kept : base + (r + 1) * kept]
                    for r in range(2 * owners)
                ]
                for s in range(square // 128):
                    w_re, w_im = weight_tiles(m, s)
                    terms = []
                    for n in range(owners):
                        re, im = adjs[2 * n], adjs[2 * n + 1]
                        terms += [re * w_re + im * w_im, im * w_re - re * w_im]
                    products[base : base + rows, s * 128 : (s + 1) * 128] = jnp.concatenate(
                        terms, axis=0
                    ).astype(bf16)
            pulled[...] += dot(products[...], gather[j])
            return 0

        lax.fori_loop(0, quads, pull, 0)
        back_copies.append(unstack_half(3, half, pulled[...]))

    for half in range(HALVES):

        def weight_terms(j, _, half=half):
            for t in range(near):
                m = (half * near + t) * quads + j
                base = t * rows
                adjs = [
                    adj_wide[half, j, base + r * kept : base + (r + 1) * kept]
                    for r in range(2 * owners)
                ]
                for s in range(square // 128):
                    lo = s * 128
                    grad_re, grad_im = None, None
                    for n in range(owners):
                        at = base + 2 * n * kept
                        re = spec_wide[half, j, at : at + kept, lo : lo + 128]
                        im = spec_wide[half, j, at + kept : at + 2 * kept, lo : lo + 128]
                        a_re, a_im = adjs[2 * n], adjs[2 * n + 1]
                        term_re = re * a_re + im * a_im
                        term_im = re * a_im - im * a_re
                        grad_re = term_re if n == 0 else grad_re + term_re
                        grad_im = term_im if n == 0 else grad_im + term_im
                    grads[m, :, lo : lo + 128] = grad_re
                    grads[m, :, square + lo : square + lo + 128] = grad_im
            return 0

        lax.fori_loop(0, quads, weight_terms, 0)
    store_grads = pltpu.make_async_copy(grads, out_grads, load_sem.at[3])
    store_grads.start()
    copies = modes_to_cells(3, 3, back_copies)
    for half in range(HALVES):
        wait_all(copies[half])
        out_cells[half] = space_recv[3 * HALVES + half]
    store_delta.wait()
    store_grads.wait()


def collect_volume(slab, half, arrived, regroup, volume, doubling):
    blocks, lanes = arrived.shape[0], arrived.shape[2]
    tile_rows = arrived.shape[1] // slab
    group = blocks * tile_rows
    pieces = []
    for block in range(blocks):
        held = arrived[block].astype(f32)
        pieces.append(
            jnp.concatenate(
                [held[x * tile_rows : (x + 1) * tile_rows] for x in range(slab)], axis=1
            )
        )
    wide = dot_nt(jnp.concatenate(pieces, axis=0).astype(bf16), regroup[...])
    quads = wide.shape[1] // lanes
    for j in range(quads):
        at = slice((half * quads + j) * group, (half * quads + j + 1) * group)
        part = wide[:, j * lanes : (j + 1) * lanes].T
        if doubling is not None:
            part = part * doubling[:, at]
        volume[:, at] = part.astype(bf16)


def result_kernel(
    slab, arrived, mix_back, regroup, delta_hbm, grads_hbm, synthesis_hbm,
    out_input, out_spectral,
    delta, grads, synthesis, volume, natural, sems, synthesis_sem,
):
    cell_rows, cells_count = delta.shape
    chunks = synthesis_sem.shape[0]
    chunk = cells_count // chunks
    width = natural.shape[1]
    lines = chunk // width
    span_y = cells_count // width
    load_delta = pltpu.make_async_copy(delta_hbm, delta, sems.at[0])
    load_delta.start()
    loads = [
        pltpu.make_async_copy(
            synthesis_hbm.at[:, pl.ds(step * chunk, chunk)],
            synthesis.at[:, pl.ds(step * chunk, chunk)],
            synthesis_sem.at[step],
        )
        for step in range(chunks)
    ]
    for copy in loads:
        copy.start()
    load_grads = pltpu.make_async_copy(grads_hbm, grads, sems.at[1])
    load_grads.start()
    for half in range(HALVES):
        collect_volume(slab, half, arrived.at[half], regroup, volume, None)
    load_delta.wait()
    for step in range(chunks):
        loads[step].wait()
        at = slice(step * chunk, (step + 1) * chunk)
        grad = dot(volume[...], synthesis[:, at]) + dot(mix_back[...], delta[:, at])
        for u in range(lines):
            natural[pl.ds(step * lines + u, cell_rows, stride=span_y), :] = grad[
                :, u * width : (u + 1) * width
            ]
    load_grads.wait()
    store_grads = pltpu.make_async_copy(grads, out_spectral, sems.at[2])
    store_grads.start()

    def narrow(step, _):
        at = pl.ds(pl.multiple_of(step * 512, 512), 512)
        out_input[at, :] = natural[at, :].astype(bf16)
        return 0

    lax.fori_loop(0, natural.shape[0] // 512, narrow, 0)
    store_grads.wait()


def fits(features, spectral, owners):
    samples, channels, slab, span_y, span_z = features.shape
    modes, kept = spectral.shape[:2]
    return (
        samples == 1 and kept == 8 and channels == 32 and slab == 4 and modes == 32
        and span_z == 128 and span_y % 8 == 0 and (2 * kept * owners) % 16 == 0
    )


def body(features, cotangent, spectral, pointwise, biases):
    blocks, owners = lax.axis_size("space"), lax.axis_size("dp")
    if not fits(features, spectral, owners):
        return plain_body(features, cotangent, spectral, pointwise, biases)
    _, channels, slab, span_y, span_z = features.shape
    modes, kept = spectral.shape[:2]
    tiles = 8
    quads = modes // tiles
    lanes = quads * channels
    square = channels * channels
    cell_rows, cells_count = channels * slab, span_y * span_z
    natural_shape = (cell_rows * span_y, span_z)
    plane, doubling = np_plane_rows(span_y, span_z, blocks, tiles, quads)
    line = np_line(slab * blocks, blocks, owners)
    plane_rows = plane.shape[0]
    chunks = 8
    rows = 2 * kept * owners
    half_rows = rows * tiles // HALVES
    sizes = (blocks, owners, channels, slab, span_y, tiles, quads, kept)
    vmem = pl.BlockSpec(memory_space=pltpu.VMEM)
    hbm = pl.BlockSpec(memory_space=pl.ANY)
    space_shape = (4 * HALVES, blocks, 2 * slab * tiles // HALVES, lanes)
    dp_shape = (4 * HALVES, owners, 2 * kept, tiles // HALVES * lanes)
    regroup, spread, gather, tile, untile, repeat = np_selectors(channels, slab, quads)
    arrived, delta, grads, mix_back = pl.pallas_call(
        functools.partial(layer_kernel, sizes),
        out_shape=(
            jax.ShapeDtypeStruct((HALVES,) + space_shape[1:], bf16),
            jax.ShapeDtypeStruct((cell_rows, cells_count), bf16),
            jax.ShapeDtypeStruct(spectral.shape, f32),
            jax.ShapeDtypeStruct((cell_rows, cell_rows), bf16),
        ),
        in_specs=[vmem, hbm, hbm, vmem, vmem] + [hbm] * 7 + [vmem] * 3,
        out_specs=(vmem, hbm, hbm, vmem),
        scratch_shapes=[
            pltpu.VMEM(natural_shape, bf16),
            pltpu.VMEM(spectral.shape, bf16),
            pltpu.VMEM((cells_count, plane_rows), bf16),
            pltpu.VMEM((plane_rows, cells_count), bf16),
            pltpu.VMEM(regroup.shape, bf16),
            pltpu.VMEM(spread.shape, bf16),
            pltpu.VMEM(gather.shape, bf16),
            pltpu.VMEM(tile.shape, bf16),
            pltpu.VMEM(untile.shape, bf16),
            pltpu.VMEM(spectral.shape, f32),
            pltpu.VMEM(natural_shape, f32),
            pltpu.VMEM((cell_rows, cells_count), bf16),
            pltpu.VMEM((cell_rows, cells_count), f32),
            pltpu.VMEM((cell_rows, cells_count), f32),
            pltpu.VMEM((cell_rows, cells_count), bf16),
            pltpu.VMEM((cell_rows, plane_rows // HALVES), f32),
            pltpu.VMEM((cell_rows, plane_rows), bf16),
            pltpu.VMEM((cell_rows, cell_rows), bf16),
            pltpu.VMEM((cell_rows, 1), f32),
            pltpu.VMEM((half_rows, lanes), bf16),
            pltpu.VMEM((quads, half_rows, lanes), bf16),
            pltpu.VMEM((HALVES, quads, half_rows, square), f32),
            pltpu.VMEM((HALVES, quads, half_rows, lanes), f32),
            pltpu.VMEM((half_rows, square), bf16),
            pltpu.VMEM((half_rows, lanes), f32),
            pltpu.VMEM((HALVES, blocks * 2 * slab * tiles // HALVES, lanes), f32),
            pltpu.VMEM(space_shape, bf16),
            pltpu.VMEM(space_shape, bf16),
            pltpu.VMEM(dp_shape, bf16),
            pltpu.VMEM(dp_shape, bf16),
            pltpu.SemaphoreType.DMA((10,)),
            pltpu.SemaphoreType.DMA((chunks,)),
            pltpu.SemaphoreType.DMA((4 * HALVES, blocks)),
            pltpu.SemaphoreType.DMA((4 * HALVES, blocks)),
            pltpu.SemaphoreType.DMA((4 * HALVES, owners)),
            pltpu.SemaphoreType.DMA((4 * HALVES, owners)),
        ],
        compiler_params=pltpu.CompilerParams(
            collective_id=0, has_side_effects=True, vmem_limit_bytes=56 * 1024 * 1024
        ),
    )(
        features.reshape(natural_shape),
        cotangent.reshape(natural_shape),
        spectral, pointwise, biases[None, :],
        np.ascontiguousarray(plane.T), plane,
        regroup, spread, gather, tile, untile, repeat, doubling.T, line,
    )
    grad_input, grad_spectral = pl.pallas_call(
        functools.partial(result_kernel, slab),
        out_shape=(
            jax.ShapeDtypeStruct(natural_shape, bf16),
            jax.ShapeDtypeStruct(spectral.shape, f32),
        ),
        in_specs=[vmem, vmem, vmem, hbm, hbm, hbm],
        out_specs=(vmem, hbm),
        scratch_shapes=[
            pltpu.VMEM((cell_rows, cells_count), bf16),
            pltpu.VMEM(spectral.shape, f32),
            pltpu.VMEM((plane_rows, cells_count), bf16),
            pltpu.VMEM((cell_rows, plane_rows), bf16),
            pltpu.VMEM(natural_shape, f32),
            pltpu.SemaphoreType.DMA((3,)),
            pltpu.SemaphoreType.DMA((chunks,)),
        ],
        compiler_params=pltpu.CompilerParams(vmem_limit_bytes=56 * 1024 * 1024),
    )(arrived, mix_back, regroup, delta, grads, plane)
    return grad_input.reshape(features.shape), grad_spectral


def solution(mesh):
    placed = (
        P("dp", None, "space", None, None),
        P("dp", None, "space", None, None),
        P("space", "dp", None),
        P(),
        P(),
    )
    return jax.shard_map(
        body,
        mesh=mesh,
        in_specs=placed,
        out_specs=(P("dp", None, "space", None, None), P("space", "dp", None)),
        check_vma=False,
    )
```

```python
import functools
import math

import jax
import jax.numpy as jnp
import ml_dtypes
import numpy as np
from jax import lax
from jax.experimental import pallas as pl
from jax.experimental.pallas import tpu as pltpu
from jax.sharding import PartitionSpec as P

KX = 32
KY = 32
KZ = 8


tanh_coef = 0.7978845608028654
cubic_coef = 0.044715


def frequencies(kept_count, length):
    indices = jnp.arange(kept_count, dtype=jnp.int32)
    return jnp.where(indices < kept_count // 2, indices, indices + (length - kept_count))


def plane_table(count_y, count_z, kept_y, kept_z):
    freq_y = frequencies(kept_y, count_y)
    freq_z = jnp.arange(kept_z, dtype=jnp.int32)
    turn_y = jnp.arange(count_y, dtype=jnp.int32)[:, None] * freq_y[None, :] % count_y
    turn_z = jnp.arange(count_z, dtype=jnp.int32)[:, None] * freq_z[None, :] % count_z
    angles = (
        2.0
        * math.pi
        * (
            turn_y[:, None, :, None].astype(jnp.float32) / count_y
            + turn_z[None, :, None, :].astype(jnp.float32) / count_z
        )
    )
    factor = 1.0 / math.sqrt(count_y * count_z)
    basis_table = jnp.stack([factor * jnp.cos(angles), -factor * jnp.sin(angles)], axis=-1)
    return basis_table.reshape(count_y * count_z, kept_y * kept_z, 2).astype(jnp.bfloat16)


def line_table(full_length, kept_count):
    freq_x = frequencies(kept_count, full_length)
    turns = jnp.arange(full_length, dtype=jnp.int32)[:, None] * freq_x[None, :] % full_length
    angles = 2.0 * math.pi * turns.astype(jnp.float32) / full_length
    factor = 1.0 / math.sqrt(full_length)
    cos_part = factor * jnp.cos(angles)
    sine_part = factor * jnp.sin(angles)
    first_row = jnp.stack([cos_part, -sine_part], axis=1)
    second = jnp.stack([sine_part, cos_part], axis=1)
    return jnp.stack([first_row, second], axis=0).astype(jnp.bfloat16)


def mode_doubling(kept_y, kept_z):
    mode_index = jnp.arange(kept_y * kept_z, dtype=jnp.int32) % kept_z
    return jnp.where(mode_index == 0, 1.0, 2.0).astype(jnp.float32)


def gelu_slope(values):
    inner_arg = tanh_coef * (values + cubic_coef * values * values * values)
    tanh_part = jnp.tanh(inner_arg)
    return 0.5 * (1.0 + tanh_part) + 0.5 * values * (1.0 - tanh_part * tanh_part) * tanh_coef * (
        1.0 + 3.0 * cubic_coef * values * values
    )


def product(equation, left_op, right_op):
    return jnp.einsum(equation, left_op, right_op, preferred_element_type=jnp.float32)


def forward_lines(coarse, line_basis):
    return product("xpscm,pxqk->kqscm", coarse, line_basis).astype(jnp.bfloat16)


def inverse_lines(spectrum, line_basis):
    return product("kqscm,pxqk->xpscm", spectrum, line_basis).astype(jnp.bfloat16)


def spectral_mix(spectrum, weights):
    real_part = spectrum[:, 0]
    imag_part = spectrum[:, 1]
    w_real = weights[:, :, 0]
    w_imag = weights[:, :, 1]
    out_real = product("ksim,mkio->ksom", real_part, w_real) - product(
        "ksim,mkio->ksom", imag_part, w_imag
    )
    out_imag = product("ksim,mkio->ksom", real_part, w_imag) + product(
        "ksim,mkio->ksom", imag_part, w_real
    )
    return jnp.stack([out_real, out_imag], axis=1).astype(jnp.bfloat16)


def spectral_pull(adjoint, weights):
    real_part = adjoint[:, 0]
    imag_part = adjoint[:, 1]
    w_real = weights[:, :, 0]
    w_imag = weights[:, :, 1]
    out_real = product("ksom,mkio->ksim", real_part, w_real) + product(
        "ksom,mkio->ksim", imag_part, w_imag
    )
    out_imag = product("ksom,mkio->ksim", imag_part, w_real) - product(
        "ksom,mkio->ksim", real_part, w_imag
    )
    return jnp.stack([out_real, out_imag], axis=1).astype(jnp.bfloat16)


def weight_grad(spectrum, adjoint):
    spec_real = spectrum[:, 0]
    spec_imag = spectrum[:, 1]
    adj_real = adjoint[:, 0]
    adj_imag = adjoint[:, 1]
    grad_real = product("ksim,ksom->mkio", spec_real, adj_real) + product(
        "ksim,ksom->mkio", spec_imag, adj_imag
    )
    grad_imag = product("ksim,ksom->mkio", spec_real, adj_imag) - product(
        "ksim,ksom->mkio", spec_imag, adj_real
    )
    return jnp.stack([grad_real, grad_imag], axis=2)


def to_modes(coarse):
    return lax.all_to_all(coarse, "space", split_axis=4, concat_axis=0, tiled=True)


def to_cells(returned):
    return lax.all_to_all(returned, "space", split_axis=0, concat_axis=4, tiled=True)


def plain_body(features, cotangent, spectral, pointwise, biases):
    samples, channels, slab_cells, span_y, span_z = features.shape
    full_length = slab_cells * lax.axis_size("space")
    plane_basis = plane_table(span_y, span_z, KY, KZ)
    line_basis = line_table(full_length, KX)
    doubling = mode_doubling(KY, KZ)
    doubling_cells = doubling.astype(jnp.bfloat16)[None, None, None, None, :]
    flat_cells = features.reshape(samples, channels, slab_cells, span_y * span_z)
    coarse = product("scxq,qmp->xpscm", flat_cells, plane_basis).astype(jnp.bfloat16)
    spectrum = forward_lines(to_modes(coarse), line_basis)
    local_modes = spectral.shape[0]
    blocks = lax.all_gather(spectral, "dp", axis=1, tiled=True)
    weights = blocks.reshape(local_modes, blocks.shape[1], 2, channels, channels)
    mixed_modes = spectral_mix(spectrum, weights)
    returned = to_cells(inverse_lines(mixed_modes, line_basis))
    spectral_part = product("xpscm,qmp->scxq", returned * doubling_cells, plane_basis)
    linear = product("sicq,io->socq", flat_cells, pointwise)
    pre_act = linear + biases.astype(jnp.float32)[None, :, None, None] + spectral_part
    upstream_grad = cotangent.reshape(flat_cells.shape).astype(jnp.float32)
    delta_cells = (upstream_grad * gelu_slope(pre_act)).astype(jnp.bfloat16)
    coarse_back = (
        product("scxq,qmp->xpscm", delta_cells, plane_basis) * doubling[None, None, None, None, :]
    ).astype(jnp.bfloat16)
    adjoint = forward_lines(to_modes(coarse_back), line_basis)
    pulled = spectral_pull(adjoint, weights)
    grad_terms = weight_grad(spectrum, adjoint)
    grad_spectral = lax.psum_scatter(
        grad_terms.reshape(local_modes, KX, 2 * channels * channels).astype(jnp.bfloat16),
        "dp",
        scatter_dimension=1,
        tiled=True,
    ).astype(jnp.float32)
    back_cells = to_cells(inverse_lines(pulled, line_basis))
    grad_cells = product("socq,io->sicq", delta_cells, pointwise) + product(
        "xpscm,qmp->scxq", back_cells, plane_basis
    )
    grad_input = grad_cells.astype(jnp.bfloat16).reshape(features.shape)
    return (grad_input, grad_spectral)


HALVES = 2


def np_frequencies(kept_count, length):
    indices = np.arange(kept_count)
    return np.where(indices < kept_count // 2, indices, indices + (length - kept_count))


def np_plane_rows(count_y, count_z, blocks, tiles, quads):
    turn_y = np.arange(count_y)[:, None] * np_frequencies(KY, count_y)[None, :] % count_y
    turn_z = np.arange(count_z)[:, None] * np.arange(KZ)[None, :] % count_z
    angles = 2.0 * np.pi * (
        turn_y[:, None, :, None] / count_y + turn_z[None, :, None, :] / count_z
    )
    factor = 1.0 / math.sqrt(count_y * count_z)
    table = np.stack([factor * np.cos(angles), -factor * np.sin(angles)], axis=0)
    near = tiles // HALVES
    table = table.reshape(2, count_y * count_z, blocks, HALVES, near, quads)
    rows = table.transpose(3, 5, 2, 0, 4, 1).reshape(-1, count_y * count_z)
    doubling = np.where(np.arange(KY * KZ) % KZ == 0, 1.0, 2.0)
    doubling = doubling.reshape(blocks, HALVES, 1, near, quads)
    doubling = np.broadcast_to(doubling, (blocks, HALVES, 2, near, quads)).transpose(1, 4, 0, 2, 3)
    return rows.astype(ml_dtypes.bfloat16), doubling.reshape(-1, 1).astype(np.float32)


def np_line(full_length, blocks, owners):
    turns = np.arange(full_length)[:, None] * np_frequencies(KX, full_length)[None, :] % full_length
    angles = 2.0 * np.pi * turns / full_length
    factor = 1.0 / math.sqrt(full_length)
    cos_part, sine_part = factor * np.cos(angles), factor * np.sin(angles)
    table = np.stack(
        [np.stack([cos_part, -sine_part], 0), np.stack([sine_part, cos_part], 0)], 0
    )
    table = table.reshape(2, 2, blocks, full_length // blocks, owners, KX // owners)
    table = table.transpose(4, 1, 5, 2, 3, 0).reshape(2 * KX, 2 * full_length)
    return table.astype(ml_dtypes.bfloat16)


def np_selectors(channels, slab, quads):
    def one_hot(rows, columns, count_rows, count_columns):
        table = np.zeros((count_rows, count_columns), ml_dtypes.bfloat16)
        table[rows.reshape(-1), columns.reshape(-1)] = 1
        return table

    lanes = quads * channels
    j, c, x = np.meshgrid(np.arange(quads), np.arange(channels), np.arange(slab), indexing="ij")
    regroup = one_hot(
        (j * channels + c) * slab + x, (x * quads + j) * channels + c, lanes * slab, lanes * slab
    )
    j, i, o = np.meshgrid(
        np.arange(quads), np.arange(channels), np.arange(channels), indexing="ij"
    )
    spread = one_hot(
        j * channels + i,
        j * channels * channels + i * channels + o,
        lanes,
        quads * channels * channels,
    )
    spread = spread.reshape(lanes, quads, channels * channels).transpose(1, 0, 2)
    j, i, o = np.meshgrid(np.arange(quads), np.arange(quads), np.arange(channels), indexing="ij")
    tile = one_hot((j * quads + i) * channels + o, j * channels + o, quads * lanes, lanes)
    cells = np.arange(channels * slab)
    repeat = one_hot(cells, cells // slab, channels * slab, channels)
    flat = np.ascontiguousarray
    return regroup, flat(spread), flat(spread.transpose(0, 2, 1)), tile, flat(tile.T), repeat


f32, bf16 = jnp.float32, jnp.bfloat16
NT = (((1,), (1,)), ((), ()))
TN = (((0,), (0,)), ((), ()))


def dot(left, right):
    return jnp.dot(left, right, preferred_element_type=f32)


def dot_nt(left, right):
    return lax.dot_general(left, right, NT, preferred_element_type=f32)


def start_exchange(axis, count, send, recv, send_sem, recv_sem):
    me = lax.axis_index(axis)
    copies = []
    for step in range(1, count):
        peer = lax.rem(me + step, count)
        copy = pltpu.make_async_remote_copy(
            src_ref=send.at[peer],
            dst_ref=recv.at[me],
            send_sem=send_sem.at[step],
            recv_sem=recv_sem.at[step],
            device_id={axis: peer},
            device_id_type=pl.DeviceIdType.MESH,
        )
        copy.start()
        copies.append(copy)
    recv[me] = send[me]
    return copies


def wait_all(copies):
    for copy in copies:
        copy.wait()


def layer_kernel(
    sizes,
    feats, cot_hbm, weights_hbm, pointwise, biases, analysis_hbm, synthesis_hbm,
    regroup_hbm, spread_hbm, gather_hbm, tile_hbm, untile_hbm, repeat, doubling, line,
    out_cells, out_delta, out_grads, mix_back,
    cot, weights, analysis, synthesis, regroup, spread, gather, tile, untile, grads,
    rows_in, linear, upstream, delta, coarse_acc, volume, mix_fwd, bias,
    stack, parts, spec_wide, adj_wide, products, pulled, cells,
    space_send, space_recv, dp_send, dp_recv,
    load_sem, analysis_sem, space_ssem, space_rsem, dp_ssem, dp_rsem,
):
    blocks, owners, channels, slab, span_y, tiles, quads, kept = sizes
    lanes = quads * channels
    rows = 2 * kept * owners
    cell_rows = channels * slab
    width = feats.shape[2]
    cells_count = span_y * width
    chunk = analysis_hbm.shape[0] // analysis_sem.shape[0]
    chunks = cells_count // chunk
    near = tiles // HALVES
    group = blocks * 2 * near
    part_columns = quads * group
    square = channels * channels
    mesh_id = pl.DeviceIdType.MESH

    analysis_loads = [
        pltpu.make_async_copy(
            analysis_hbm.at[pl.ds(step * chunk, chunk)],
            analysis.at[pl.ds(step * chunk, chunk)],
            analysis_sem.at[step],
        )
        for step in range(chunks)
    ]
    for copy in analysis_loads:
        copy.start()
    load_cot = pltpu.make_async_copy(cot_hbm, cot, load_sem.at[0])
    load_weights = pltpu.make_async_copy(weights_hbm, weights, load_sem.at[1])
    load_synthesis = pltpu.make_async_copy(synthesis_hbm, synthesis, load_sem.at[2])
    load_tables = [
        pltpu.make_async_copy(source, target, load_sem.at[5 + at])
        for at, (source, target) in enumerate(
            [(regroup_hbm, regroup), (spread_hbm, spread), (tile_hbm, tile),
             (untile_hbm, untile), (gather_hbm, gather)]
        )
    ]
    load_tables[0].start()
    load_cot.start()
    load_weights.start()
    for copy in load_tables[1:]:
        copy.start()
    load_synthesis.start()

    barrier = pltpu.get_barrier_semaphore()
    for axis, count in (("space", blocks), ("dp", owners)):
        me = lax.axis_index(axis)
        for step in range(1, count):
            pl.semaphore_signal(
                barrier, inc=1, device_id={axis: lax.rem(me + step, count)}, device_id_type=mesh_id
            )

    def to_lines(source, target):
        def some(step, _):
            at = pl.ds(pl.multiple_of(step * 16, 16), 16)
            swapped = jnp.swapaxes(source[at].astype(f32), 0, 1)
            for y in range(span_y):
                target[at, y * width : (y + 1) * width] = swapped[y].astype(target.dtype)
            return 0

        lax.fori_loop(0, cell_rows // 16, some, 0)

    def columns(step):
        return pl.ds(pl.multiple_of(step * chunk, chunk), chunk)

    def send_space(turn, half):
        at = turn * HALVES + half
        return start_exchange(
            "space", blocks, space_send.at[at], space_recv.at[at],
            space_ssem.at[at], space_rsem.at[at],
        )

    def send_dp(turn, half):
        at = turn * HALVES + half
        return start_exchange(
            "dp", owners, dp_send.at[at], dp_recv.at[at], dp_ssem.at[at], dp_rsem.at[at]
        )

    def send_cells(turn, half, coarse):
        wide = jnp.concatenate(
            [coarse[:, j * group : (j + 1) * group].T.astype(bf16) for j in range(quads)], axis=1
        )
        wide = dot(wide, regroup[...])
        for block in range(blocks):
            at = block * 2 * near
            pieces = [wide[at : at + 2 * near, x * lanes : (x + 1) * lanes] for x in range(slab)]
            space_send[turn * HALVES + half, block] = jnp.concatenate(pieces, axis=0).astype(bf16)
        return send_space(turn, half)

    def cells_to_modes(turn, dp_turn, arriving):
        copies = []
        for half in range(HALVES):
            wait_all(arriving[half])
            cells[half] = space_recv[turn * HALVES + half].astype(f32).reshape(cells.shape[1:])
            wide = jnp.concatenate(
                [cells[half, pl.ds(t, blocks * 2 * slab, stride=near), :] for t in range(near)],
                axis=1,
            ).astype(bf16)
            spectrum = dot(line[...], wide).astype(bf16)
            dp_send[dp_turn * HALVES + half] = spectrum.reshape(owners, 2 * kept, near * lanes)
            copies.append(send_dp(dp_turn, half))
        return copies

    def modes_to_cells(dp_turn, turn, arriving):
        copies = []
        for half in range(HALVES):
            wait_all(arriving[half])
            wide = dp_recv[dp_turn * HALVES + half].reshape(rows, near * lanes)
            back = lax.dot_general(line[...], wide, TN, preferred_element_type=f32)
            for t in range(near):
                cells[half, pl.ds(t, blocks * 2 * slab, stride=near), :] = back[
                    :, t * lanes : (t + 1) * lanes
                ]
            space_send[turn * HALVES + half] = (
                cells[half].astype(bf16).reshape(space_send.shape[1:])
            )
            copies.append(send_space(turn, half))
        return copies

    def stack_half(dp_turn, half):
        for t in range(near):
            stack[t * rows : (t + 1) * rows] = dp_recv[
                dp_turn * HALVES + half, :, :, t * lanes : (t + 1) * lanes
            ].reshape(rows, lanes)

    def unstack_half(dp_turn, half, values):
        for t in range(near):
            dp_send[dp_turn * HALVES + half, :, :, t * lanes : (t + 1) * lanes] = (
                values[t * rows : (t + 1) * rows].astype(bf16).reshape(owners, 2 * kept, lanes)
            )
        return send_dp(dp_turn, half)

    def weight_tiles(m, s):
        lo = s * 128
        return (
            weights[m, :, lo : lo + 128].astype(f32),
            weights[m, :, square + lo : square + lo + 128].astype(f32),
        )

    to_lines(feats, rows_in)

    def analyse(half, source):
        at = slice(half * part_columns, (half + 1) * part_columns)
        coarse_acc[...] = jnp.zeros_like(coarse_acc)
        for step in range(chunks):
            if half == 0 and source is rows_in:
                analysis_loads[step].wait()
            rows_at = slice(step * chunk, (step + 1) * chunk)
            coarse_acc[...] += dot(source[:, rows_at], analysis[rows_at, at])
        return coarse_acc[...]

    coarse = analyse(0, rows_in)
    pl.semaphore_wait(barrier, blocks + owners - 2)
    load_tables[0].wait()
    copies = [send_cells(0, 0, coarse)]
    for half in range(1, HALVES):
        copies.append(send_cells(0, half, analyse(half, rows_in)))

    same_cell = lax.rem(lax.broadcasted_iota(jnp.int32, mix_fwd.shape, 0), slab) == lax.rem(
        lax.broadcasted_iota(jnp.int32, mix_fwd.shape, 1), slab
    )
    spread_out = dot_nt(dot_nt(repeat[...], pointwise[...]).astype(bf16), repeat[...])
    mix_fwd[...] = jnp.where(same_cell, spread_out, 0.0).astype(bf16)
    spread_out = dot_nt(dot(repeat[...], pointwise[...]).astype(bf16), repeat[...])
    mix_back[...] = jnp.where(same_cell, spread_out, 0.0).astype(bf16)
    bias[...] = jnp.sum(
        repeat[...].astype(f32) * biases[...].astype(f32), axis=1, keepdims=True
    )
    load_cot.wait()
    to_lines(cot, upstream)

    def prepare(step, _):
        at = columns(step)
        linear[:, at] = dot(mix_fwd[...], rows_in[:, at]) + bias[...]
        return 0

    lax.fori_loop(0, chunks, prepare, 0)
    copies = cells_to_modes(0, 0, copies)
    load_weights.wait()
    for copy in load_tables[1:]:
        copy.wait()

    back_copies = []
    for half in range(HALVES):
        wait_all(copies[half])
        stack_half(0, half)

        def mix(j, _, half=half):
            spec_wide[half, j] = dot(stack[...], spread[j])
            for t in range(near):
                m = (half * near + t) * quads + j
                base = t * rows
                total = [None] * (2 * owners)
                for s in range(square // 128):
                    lo = s * 128
                    w_re, w_im = weight_tiles(m, s)
                    for n in range(owners):
                        at = base + 2 * n * kept
                        re = spec_wide[half, j, at : at + kept, lo : lo + 128]
                        im = spec_wide[half, j, at + kept : at + 2 * kept, lo : lo + 128]
                        out_re = re * w_re - im * w_im
                        out_im = re * w_im + im * w_re
                        total[2 * n] = out_re if s == 0 else total[2 * n] + out_re
                        total[2 * n + 1] = out_im if s == 0 else total[2 * n + 1] + out_im
                parts[j, base : base + rows, :] = jnp.concatenate(total, axis=0).astype(bf16)
            return 0

        lax.fori_loop(0, quads, mix, 0)
        mixed = dot(jnp.concatenate([parts[j] for j in range(quads)], axis=1), tile[...])
        back_copies.append(unstack_half(1, half, mixed))
    copies = modes_to_cells(1, 1, back_copies)
    load_synthesis.wait()
    for half in range(HALVES):
        wait_all(copies[half])
        collect_volume(
            slab, half, space_recv.at[HALVES + half], regroup, volume, doubling
        )

    def activate(step, _):
        at = columns(step)
        pre_act = dot(volume[...], synthesis[:, at]) + linear[:, at]
        delta[:, at] = (upstream[:, at] * gelu_slope(pre_act)).astype(bf16)
        return 0

    lax.fori_loop(0, chunks, activate, 0)
    copies = []
    for half in range(HALVES):
        at = slice(half * part_columns, (half + 1) * part_columns)
        copies.append(send_cells(2, half, analyse(half, delta) * doubling[:, at]))
    store_delta = pltpu.make_async_copy(delta, out_delta, load_sem.at[4])
    store_delta.start()
    copies = cells_to_modes(2, 2, copies)

    back_copies = []
    for half in range(HALVES):
        wait_all(copies[half])
        stack_half(2, half)
        wide = dot(stack[...], untile[...])
        for j in range(quads):
            adj_wide[half, j] = wide[:, j * lanes : (j + 1) * lanes]
        pulled[...] = jnp.zeros_like(pulled)

        def pull(j, _, half=half):
            for t in range(near):
                m = (half * near + t) * quads + j
                base = t * rows
                adjs = [
                    adj_wide[half, j, base + r * kept : base + (r + 1) * kept]
                    for r in range(2 * owners)
                ]
                for s in range(square // 128):
                    w_re, w_im = weight_tiles(m, s)
                    terms = []
                    for n in range(owners):
                        re, im = adjs[2 * n], adjs[2 * n + 1]
                        terms += [re * w_re + im * w_im, im * w_re - re * w_im]
                    products[base : base + rows, s * 128 : (s + 1) * 128] = jnp.concatenate(
                        terms, axis=0
                    ).astype(bf16)
            pulled[...] += dot(products[...], gather[j])
            return 0

        lax.fori_loop(0, quads, pull, 0)
        back_copies.append(unstack_half(3, half, pulled[...]))

    for half in range(HALVES):

        def weight_terms(j, _, half=half):
            for t in range(near):
                m = (half * near + t) * quads + j
                base = t * rows
                adjs = [
                    adj_wide[half, j, base + r * kept : base + (r + 1) * kept]
                    for r in range(2 * owners)
                ]
                for s in range(square // 128):
                    lo = s * 128
                    grad_re, grad_im = None, None
                    for n in range(owners):
                        at = base + 2 * n * kept
                        re = spec_wide[half, j, at : at + kept, lo : lo + 128]
                        im = spec_wide[half, j, at + kept : at + 2 * kept, lo : lo + 128]
                        a_re, a_im = adjs[2 * n], adjs[2 * n + 1]
                        term_re = re * a_re + im * a_im
                        term_im = re * a_im - im * a_re
                        grad_re = term_re if n == 0 else grad_re + term_re
                        grad_im = term_im if n == 0 else grad_im + term_im
                    grads[m, :, lo : lo + 128] = grad_re
                    grads[m, :, square + lo : square + lo + 128] = grad_im
            return 0

        lax.fori_loop(0, quads, weight_terms, 0)
    store_grads = pltpu.make_async_copy(grads, out_grads, load_sem.at[3])
    store_grads.start()
    copies = modes_to_cells(3, 3, back_copies)
    for half in range(HALVES):
        wait_all(copies[half])
        out_cells[half] = space_recv[3 * HALVES + half]
    store_delta.wait()
    store_grads.wait()


def collect_volume(slab, half, arrived, regroup, volume, doubling):
    blocks, lanes = arrived.shape[0], arrived.shape[2]
    tile_rows = arrived.shape[1] // slab
    group = blocks * tile_rows
    pieces = []
    for block in range(blocks):
        held = arrived[block].astype(f32)
        pieces.append(
            jnp.concatenate(
                [held[x * tile_rows : (x + 1) * tile_rows] for x in range(slab)], axis=1
            )
        )
    wide = dot_nt(jnp.concatenate(pieces, axis=0).astype(bf16), regroup[...])
    quads = wide.shape[1] // lanes
    for j in range(quads):
        at = slice((half * quads + j) * group, (half * quads + j + 1) * group)
        part = wide[:, j * lanes : (j + 1) * lanes].T
        if doubling is not None:
            part = part * doubling[:, at]
        volume[:, at] = part.astype(bf16)


def result_kernel(
    slab, arrived, mix_back, regroup, delta_hbm, grads_hbm, synthesis_hbm,
    out_input, out_spectral,
    delta, grads, synthesis, volume, lined, natural, sems, synthesis_sem, out_sem,
):
    cell_rows, cells_count = delta.shape
    chunks = synthesis_sem.shape[0]
    chunk = cells_count // chunks
    span_y, width = natural.shape[1:]
    load_delta = pltpu.make_async_copy(delta_hbm, delta, sems.at[0])
    load_delta.start()
    loads = [
        pltpu.make_async_copy(
            synthesis_hbm.at[:, pl.ds(step * chunk, chunk)],
            synthesis.at[:, pl.ds(step * chunk, chunk)],
            synthesis_sem.at[step],
        )
        for step in range(chunks)
    ]
    for copy in loads:
        copy.start()
    load_grads = pltpu.make_async_copy(grads_hbm, grads, sems.at[1])
    load_grads.start()
    for half in range(HALVES):
        collect_volume(slab, half, arrived.at[half], regroup, volume, None)
    load_delta.wait()
    parts = out_sem.shape[0]
    part_y = span_y // parts
    stores = []
    for part in range(parts):
        for step in range(part * chunks // parts, (part + 1) * chunks // parts):
            loads[step].wait()
            at = slice(step * chunk, (step + 1) * chunk)
            lined[:, at] = dot(volume[...], synthesis[:, at]) + dot(mix_back[...], delta[:, at])

        def swap(step, _, part=part):
            at = pl.ds(pl.multiple_of(step * 8, 8), 8)
            stacked = jnp.stack(
                [
                    lined[at, y * width : (y + 1) * width]
                    for y in range(part * part_y, (part + 1) * part_y)
                ],
                axis=0,
            )
            natural[at, part * part_y : (part + 1) * part_y, :] = jnp.swapaxes(
                stacked, 0, 1
            ).astype(bf16)
            return 0

        lax.fori_loop(0, cell_rows // 8, swap, 0)
        copy = pltpu.make_async_copy(
            natural.at[:, pl.ds(part * part_y, part_y), :],
            out_input.at[:, pl.ds(part * part_y, part_y), :],
            out_sem.at[part],
        )
        copy.start()
        stores.append(copy)
        if part == 0:
            load_grads.wait()
            store_grads = pltpu.make_async_copy(grads, out_spectral, sems.at[2])
            store_grads.start()
            stores.append(store_grads)
    wait_all(stores)


def fits(features, spectral, owners):
    samples, channels, slab, span_y, span_z = features.shape
    modes, kept = spectral.shape[:2]
    return (
        samples == 1 and kept == 8 and channels == 32 and slab == 4 and modes == 32
        and span_z == 128 and span_y % 16 == 0 and (2 * kept * owners) % 16 == 0
    )


def body(features, cotangent, spectral, pointwise, biases):
    blocks, owners = lax.axis_size("space"), lax.axis_size("dp")
    if not fits(features, spectral, owners):
        return plain_body(features, cotangent, spectral, pointwise, biases)
    _, channels, slab, span_y, span_z = features.shape
    modes, kept = spectral.shape[:2]
    tiles = 8
    quads = modes // tiles
    lanes = quads * channels
    square = channels * channels
    cell_rows, cells_count = channels * slab, span_y * span_z
    natural_shape = (cell_rows, span_y, span_z)
    plane, doubling = np_plane_rows(span_y, span_z, blocks, tiles, quads)
    line = np_line(slab * blocks, blocks, owners)
    plane_rows = plane.shape[0]
    chunks = 8
    rows = 2 * kept * owners
    half_rows = rows * tiles // HALVES
    sizes = (blocks, owners, channels, slab, span_y, tiles, quads, kept)
    vmem = pl.BlockSpec(memory_space=pltpu.VMEM)
    hbm = pl.BlockSpec(memory_space=pl.ANY)
    space_shape = (4 * HALVES, blocks, 2 * slab * tiles // HALVES, lanes)
    dp_shape = (4 * HALVES, owners, 2 * kept, tiles // HALVES * lanes)
    regroup, spread, gather, tile, untile, repeat = np_selectors(channels, slab, quads)
    arrived, delta, grads, mix_back = pl.pallas_call(
        functools.partial(layer_kernel, sizes),
        out_shape=(
            jax.ShapeDtypeStruct((HALVES,) + space_shape[1:], bf16),
            jax.ShapeDtypeStruct((cell_rows, cells_count), bf16),
            jax.ShapeDtypeStruct(spectral.shape, f32),
            jax.ShapeDtypeStruct((cell_rows, cell_rows), bf16),
        ),
        in_specs=[vmem, hbm, hbm, vmem, vmem] + [hbm] * 7 + [vmem] * 3,
        out_specs=(vmem, hbm, hbm, vmem),
        scratch_shapes=[
            pltpu.VMEM(natural_shape, bf16),
            pltpu.VMEM(spectral.shape, bf16),
            pltpu.VMEM((cells_count, plane_rows), bf16),
            pltpu.VMEM((plane_rows, cells_count), bf16),
            pltpu.VMEM(regroup.shape, bf16),
            pltpu.VMEM(spread.shape, bf16),
            pltpu.VMEM(gather.shape, bf16),
            pltpu.VMEM(tile.shape, bf16),
            pltpu.VMEM(untile.shape, bf16),
            pltpu.VMEM(spectral.shape, f32),
            pltpu.VMEM((cell_rows, cells_count), bf16),
            pltpu.VMEM((cell_rows, cells_count), f32),
            pltpu.VMEM((cell_rows, cells_count), f32),
            pltpu.VMEM((cell_rows, cells_count), bf16),
            pltpu.VMEM((cell_rows, plane_rows // HALVES), f32),
            pltpu.VMEM((cell_rows, plane_rows), bf16),
            pltpu.VMEM((cell_rows, cell_rows), bf16),
            pltpu.VMEM((cell_rows, 1), f32),
            pltpu.VMEM((half_rows, lanes), bf16),
            pltpu.VMEM((quads, half_rows, lanes), bf16),
            pltpu.VMEM((HALVES, quads, half_rows, square), f32),
            pltpu.VMEM((HALVES, quads, half_rows, lanes), f32),
            pltpu.VMEM((half_rows, square), bf16),
            pltpu.VMEM((half_rows, lanes), f32),
            pltpu.VMEM((HALVES, blocks * 2 * slab * tiles // HALVES, lanes), f32),
            pltpu.VMEM(space_shape, bf16),
            pltpu.VMEM(space_shape, bf16),
            pltpu.VMEM(dp_shape, bf16),
            pltpu.VMEM(dp_shape, bf16),
            pltpu.SemaphoreType.DMA((10,)),
            pltpu.SemaphoreType.DMA((chunks,)),
            pltpu.SemaphoreType.DMA((4 * HALVES, blocks)),
            pltpu.SemaphoreType.DMA((4 * HALVES, blocks)),
            pltpu.SemaphoreType.DMA((4 * HALVES, owners)),
            pltpu.SemaphoreType.DMA((4 * HALVES, owners)),
        ],
        compiler_params=pltpu.CompilerParams(
            collective_id=0, has_side_effects=True, vmem_limit_bytes=56 * 1024 * 1024
        ),
    )(
        features.reshape(natural_shape),
        cotangent.reshape(natural_shape),
        spectral, pointwise, biases[None, :],
        np.ascontiguousarray(plane.T), plane,
        regroup, spread, gather, tile, untile, repeat, doubling.T, line,
    )
    grad_input, grad_spectral = pl.pallas_call(
        functools.partial(result_kernel, slab),
        out_shape=(
            jax.ShapeDtypeStruct(natural_shape, bf16),
            jax.ShapeDtypeStruct(spectral.shape, f32),
        ),
        in_specs=[vmem, vmem, vmem, hbm, hbm, hbm],
        out_specs=(hbm, hbm),
        scratch_shapes=[
            pltpu.VMEM((cell_rows, cells_count), bf16),
            pltpu.VMEM(spectral.shape, f32),
            pltpu.VMEM((plane_rows, cells_count), bf16),
            pltpu.VMEM((cell_rows, plane_rows), bf16),
            pltpu.VMEM((cell_rows, cells_count), f32),
            pltpu.VMEM(natural_shape, bf16),
            pltpu.SemaphoreType.DMA((3,)),
            pltpu.SemaphoreType.DMA((chunks,)),
            pltpu.SemaphoreType.DMA((span_y // 16,)),
        ],
        compiler_params=pltpu.CompilerParams(vmem_limit_bytes=56 * 1024 * 1024),
    )(arrived, mix_back, regroup, delta, grads, plane)
    return grad_input.reshape(features.shape), grad_spectral


def solution(mesh):
    placed = (
        P("dp", None, "space", None, None),
        P("dp", None, "space", None, None),
        P("space", "dp", None),
        P(),
        P(),
    )
    return jax.shard_map(
        body,
        mesh=mesh,
        in_specs=placed,
        out_specs=(P("dp", None, "space", None, None), P("space", "dp", None)),
        check_vma=False,
    )
```

```python
import functools
import math

import jax
import jax.numpy as jnp
import ml_dtypes
import numpy as np
from jax import lax
from jax.experimental import pallas as pl
from jax.experimental.pallas import tpu as pltpu
from jax.sharding import PartitionSpec as P

KX = 32
KY = 32
KZ = 8


tanh_coef = 0.7978845608028654
cubic_coef = 0.044715


def frequencies(kept_count, length):
    indices = jnp.arange(kept_count, dtype=jnp.int32)
    return jnp.where(indices < kept_count // 2, indices, indices + (length - kept_count))


def plane_table(count_y, count_z, kept_y, kept_z):
    freq_y = frequencies(kept_y, count_y)
    freq_z = jnp.arange(kept_z, dtype=jnp.int32)
    turn_y = jnp.arange(count_y, dtype=jnp.int32)[:, None] * freq_y[None, :] % count_y
    turn_z = jnp.arange(count_z, dtype=jnp.int32)[:, None] * freq_z[None, :] % count_z
    angles = (
        2.0
        * math.pi
        * (
            turn_y[:, None, :, None].astype(jnp.float32) / count_y
            + turn_z[None, :, None, :].astype(jnp.float32) / count_z
        )
    )
    factor = 1.0 / math.sqrt(count_y * count_z)
    basis_table = jnp.stack([factor * jnp.cos(angles), -factor * jnp.sin(angles)], axis=-1)
    return basis_table.reshape(count_y * count_z, kept_y * kept_z, 2).astype(jnp.bfloat16)


def line_table(full_length, kept_count):
    freq_x = frequencies(kept_count, full_length)
    turns = jnp.arange(full_length, dtype=jnp.int32)[:, None] * freq_x[None, :] % full_length
    angles = 2.0 * math.pi * turns.astype(jnp.float32) / full_length
    factor = 1.0 / math.sqrt(full_length)
    cos_part = factor * jnp.cos(angles)
    sine_part = factor * jnp.sin(angles)
    first_row = jnp.stack([cos_part, -sine_part], axis=1)
    second = jnp.stack([sine_part, cos_part], axis=1)
    return jnp.stack([first_row, second], axis=0).astype(jnp.bfloat16)


def mode_doubling(kept_y, kept_z):
    mode_index = jnp.arange(kept_y * kept_z, dtype=jnp.int32) % kept_z
    return jnp.where(mode_index == 0, 1.0, 2.0).astype(jnp.float32)


def gelu_slope(values):
    inner_arg = tanh_coef * (values + cubic_coef * values * values * values)
    tanh_part = jnp.tanh(inner_arg)
    return 0.5 * (1.0 + tanh_part) + 0.5 * values * (1.0 - tanh_part * tanh_part) * tanh_coef * (
        1.0 + 3.0 * cubic_coef * values * values
    )


def product(equation, left_op, right_op):
    return jnp.einsum(equation, left_op, right_op, preferred_element_type=jnp.float32)


def forward_lines(coarse, line_basis):
    return product("xpscm,pxqk->kqscm", coarse, line_basis).astype(jnp.bfloat16)


def inverse_lines(spectrum, line_basis):
    return product("kqscm,pxqk->xpscm", spectrum, line_basis).astype(jnp.bfloat16)


def spectral_mix(spectrum, weights):
    real_part = spectrum[:, 0]
    imag_part = spectrum[:, 1]
    w_real = weights[:, :, 0]
    w_imag = weights[:, :, 1]
    out_real = product("ksim,mkio->ksom", real_part, w_real) - product(
        "ksim,mkio->ksom", imag_part, w_imag
    )
    out_imag = product("ksim,mkio->ksom", real_part, w_imag) + product(
        "ksim,mkio->ksom", imag_part, w_real
    )
    return jnp.stack([out_real, out_imag], axis=1).astype(jnp.bfloat16)


def spectral_pull(adjoint, weights):
    real_part = adjoint[:, 0]
    imag_part = adjoint[:, 1]
    w_real = weights[:, :, 0]
    w_imag = weights[:, :, 1]
    out_real = product("ksom,mkio->ksim", real_part, w_real) + product(
        "ksom,mkio->ksim", imag_part, w_imag
    )
    out_imag = product("ksom,mkio->ksim", imag_part, w_real) - product(
        "ksom,mkio->ksim", real_part, w_imag
    )
    return jnp.stack([out_real, out_imag], axis=1).astype(jnp.bfloat16)


def weight_grad(spectrum, adjoint):
    spec_real = spectrum[:, 0]
    spec_imag = spectrum[:, 1]
    adj_real = adjoint[:, 0]
    adj_imag = adjoint[:, 1]
    grad_real = product("ksim,ksom->mkio", spec_real, adj_real) + product(
        "ksim,ksom->mkio", spec_imag, adj_imag
    )
    grad_imag = product("ksim,ksom->mkio", spec_real, adj_imag) - product(
        "ksim,ksom->mkio", spec_imag, adj_real
    )
    return jnp.stack([grad_real, grad_imag], axis=2)


def to_modes(coarse):
    return lax.all_to_all(coarse, "space", split_axis=4, concat_axis=0, tiled=True)


def to_cells(returned):
    return lax.all_to_all(returned, "space", split_axis=0, concat_axis=4, tiled=True)


def plain_body(features, cotangent, spectral, pointwise, biases):
    samples, channels, slab_cells, span_y, span_z = features.shape
    full_length = slab_cells * lax.axis_size("space")
    plane_basis = plane_table(span_y, span_z, KY, KZ)
    line_basis = line_table(full_length, KX)
    doubling = mode_doubling(KY, KZ)
    doubling_cells = doubling.astype(jnp.bfloat16)[None, None, None, None, :]
    flat_cells = features.reshape(samples, channels, slab_cells, span_y * span_z)
    coarse = product("scxq,qmp->xpscm", flat_cells, plane_basis).astype(jnp.bfloat16)
    spectrum = forward_lines(to_modes(coarse), line_basis)
    local_modes = spectral.shape[0]
    blocks = lax.all_gather(spectral, "dp", axis=1, tiled=True)
    weights = blocks.reshape(local_modes, blocks.shape[1], 2, channels, channels)
    mixed_modes = spectral_mix(spectrum, weights)
    returned = to_cells(inverse_lines(mixed_modes, line_basis))
    spectral_part = product("xpscm,qmp->scxq", returned * doubling_cells, plane_basis)
    linear = product("sicq,io->socq", flat_cells, pointwise)
    pre_act = linear + biases.astype(jnp.float32)[None, :, None, None] + spectral_part
    upstream_grad = cotangent.reshape(flat_cells.shape).astype(jnp.float32)
    delta_cells = (upstream_grad * gelu_slope(pre_act)).astype(jnp.bfloat16)
    coarse_back = (
        product("scxq,qmp->xpscm", delta_cells, plane_basis) * doubling[None, None, None, None, :]
    ).astype(jnp.bfloat16)
    adjoint = forward_lines(to_modes(coarse_back), line_basis)
    pulled = spectral_pull(adjoint, weights)
    grad_terms = weight_grad(spectrum, adjoint)
    grad_spectral = lax.psum_scatter(
        grad_terms.reshape(local_modes, KX, 2 * channels * channels).astype(jnp.bfloat16),
        "dp",
        scatter_dimension=1,
        tiled=True,
    ).astype(jnp.float32)
    back_cells = to_cells(inverse_lines(pulled, line_basis))
    grad_cells = product("socq,io->sicq", delta_cells, pointwise) + product(
        "xpscm,qmp->scxq", back_cells, plane_basis
    )
    grad_input = grad_cells.astype(jnp.bfloat16).reshape(features.shape)
    return (grad_input, grad_spectral)


HALVES = 2


def np_frequencies(kept_count, length):
    indices = np.arange(kept_count)
    return np.where(indices < kept_count // 2, indices, indices + (length - kept_count))


def np_plane_rows(count_y, count_z, blocks, tiles, quads):
    turn_y = np.arange(count_y)[:, None] * np_frequencies(KY, count_y)[None, :] % count_y
    turn_z = np.arange(count_z)[:, None] * np.arange(KZ)[None, :] % count_z
    angles = 2.0 * np.pi * (
        turn_y[:, None, :, None] / count_y + turn_z[None, :, None, :] / count_z
    )
    factor = 1.0 / math.sqrt(count_y * count_z)
    table = np.stack([factor * np.cos(angles), -factor * np.sin(angles)], axis=0)
    near = tiles // HALVES
    table = table.reshape(2, count_y * count_z, blocks, HALVES, near, quads)
    rows = table.transpose(3, 5, 2, 0, 4, 1).reshape(-1, count_y * count_z)
    doubling = np.where(np.arange(KY * KZ) % KZ == 0, 1.0, 2.0)
    doubling = doubling.reshape(blocks, HALVES, 1, near, quads)
    doubling = np.broadcast_to(doubling, (blocks, HALVES, 2, near, quads)).transpose(1, 4, 0, 2, 3)
    return rows.astype(ml_dtypes.bfloat16), doubling.reshape(-1, 1).astype(np.float32)


def np_line(full_length, blocks, owners):
    turns = np.arange(full_length)[:, None] * np_frequencies(KX, full_length)[None, :] % full_length
    angles = 2.0 * np.pi * turns / full_length
    factor = 1.0 / math.sqrt(full_length)
    cos_part, sine_part = factor * np.cos(angles), factor * np.sin(angles)
    table = np.stack(
        [np.stack([cos_part, -sine_part], 0), np.stack([sine_part, cos_part], 0)], 0
    )
    table = table.reshape(2, 2, blocks, full_length // blocks, owners, KX // owners)
    table = table.transpose(4, 1, 5, 2, 3, 0).reshape(2 * KX, 2 * full_length)
    return table.astype(ml_dtypes.bfloat16)


def np_selectors(channels, slab, quads):
    def one_hot(rows, columns, count_rows, count_columns):
        table = np.zeros((count_rows, count_columns), ml_dtypes.bfloat16)
        table[rows.reshape(-1), columns.reshape(-1)] = 1
        return table

    lanes = quads * channels
    j, c, x = np.meshgrid(np.arange(quads), np.arange(channels), np.arange(slab), indexing="ij")
    regroup = one_hot(
        (j * channels + c) * slab + x, (x * quads + j) * channels + c, lanes * slab, lanes * slab
    )
    j, i, o = np.meshgrid(
        np.arange(quads), np.arange(channels), np.arange(channels), indexing="ij"
    )
    spread = one_hot(
        j * channels + i,
        j * channels * channels + i * channels + o,
        lanes,
        quads * channels * channels,
    )
    spread = spread.reshape(lanes, quads, channels * channels).transpose(1, 0, 2)
    j, i, o = np.meshgrid(np.arange(quads), np.arange(quads), np.arange(channels), indexing="ij")
    tile = one_hot((j * quads + i) * channels + o, j * channels + o, quads * lanes, lanes)
    cells = np.arange(channels * slab)
    repeat = one_hot(cells, cells // slab, channels * slab, channels)
    flat = np.ascontiguousarray
    return regroup, flat(spread), flat(spread.transpose(0, 2, 1)), tile, flat(tile.T), repeat


f32, bf16 = jnp.float32, jnp.bfloat16
NT = (((1,), (1,)), ((), ()))
TN = (((0,), (0,)), ((), ()))


def dot(left, right):
    return jnp.dot(left, right, preferred_element_type=f32)


def dot_nt(left, right):
    return lax.dot_general(left, right, NT, preferred_element_type=f32)


def start_exchange(axis, count, send, recv, send_sem, recv_sem):
    me = lax.axis_index(axis)
    copies = []
    for step in range(1, count):
        peer = lax.rem(me + step, count)
        copy = pltpu.make_async_remote_copy(
            src_ref=send.at[peer],
            dst_ref=recv.at[me],
            send_sem=send_sem.at[step],
            recv_sem=recv_sem.at[step],
            device_id={axis: peer},
            device_id_type=pl.DeviceIdType.MESH,
        )
        copy.start()
        copies.append(copy)
    recv[me] = send[me]
    return copies


def wait_all(copies):
    for copy in copies:
        copy.wait()


def wait_arrivals(copies):
    for copy in copies:
        copy.wait_recv()


def layer_kernel(
    sizes,
    feats, cot_hbm, weights_hbm, pointwise, biases, analysis_hbm, synthesis_hbm,
    regroup_hbm, spread_hbm, gather_hbm, tile_hbm, untile_hbm, repeat, doubling, line,
    out_cells, out_delta, out_grads, mix_back,
    cot, weights, analysis, synthesis, regroup, spread, gather, tile, untile, grads,
    rows_in, linear, upstream, delta, coarse_acc, volume, mix_fwd, bias,
    stack, parts, spec_wide, adj_wide, products, pulled, cells,
    space_send, space_recv, dp_send, dp_recv,
    load_sem, analysis_sem, space_ssem, space_rsem, dp_ssem, dp_rsem,
):
    blocks, owners, channels, slab, span_y, tiles, quads, kept = sizes
    lanes = quads * channels
    rows = 2 * kept * owners
    cell_rows = channels * slab
    width = feats.shape[2]
    cells_count = span_y * width
    chunk = analysis_hbm.shape[0] // analysis_sem.shape[0]
    chunks = cells_count // chunk
    near = tiles // HALVES
    group = blocks * 2 * near
    part_columns = quads * group
    square = channels * channels
    mesh_id = pl.DeviceIdType.MESH

    analysis_loads = [
        pltpu.make_async_copy(
            analysis_hbm.at[pl.ds(step * chunk, chunk)],
            analysis.at[pl.ds(step * chunk, chunk)],
            analysis_sem.at[step],
        )
        for step in range(chunks)
    ]
    for copy in analysis_loads:
        copy.start()
    load_cot = pltpu.make_async_copy(cot_hbm, cot, load_sem.at[0])
    load_weights = pltpu.make_async_copy(weights_hbm, weights, load_sem.at[1])
    load_synthesis = pltpu.make_async_copy(synthesis_hbm, synthesis, load_sem.at[2])
    load_tables = [
        pltpu.make_async_copy(source, target, load_sem.at[5 + at])
        for at, (source, target) in enumerate(
            [(regroup_hbm, regroup), (spread_hbm, spread), (tile_hbm, tile),
             (untile_hbm, untile), (gather_hbm, gather)]
        )
    ]
    load_tables[0].start()
    load_cot.start()
    load_weights.start()
    for copy in load_tables[1:]:
        copy.start()
    load_synthesis.start()

    barrier = pltpu.get_barrier_semaphore()
    for axis, count in (("space", blocks), ("dp", owners)):
        me = lax.axis_index(axis)
        for step in range(1, count):
            pl.semaphore_signal(
                barrier, inc=1, device_id={axis: lax.rem(me + step, count)}, device_id_type=mesh_id
            )

    def to_lines(source, target):
        def some(step, _):
            at = pl.ds(pl.multiple_of(step * 16, 16), 16)
            swapped = jnp.swapaxes(source[at].astype(f32), 0, 1)
            for y in range(span_y):
                target[at, y * width : (y + 1) * width] = swapped[y].astype(target.dtype)
            return 0

        lax.fori_loop(0, cell_rows // 16, some, 0)

    def columns(step):
        return pl.ds(pl.multiple_of(step * chunk, chunk), chunk)

    sent = []

    def sending(*exchange):
        copies = start_exchange(*exchange)
        sent.extend(copies)
        return copies

    def send_space(turn, half):
        at = turn * HALVES + half
        return sending(
            "space", blocks, space_send.at[at], space_recv.at[at],
            space_ssem.at[at], space_rsem.at[at],
        )

    def send_dp(turn, half):
        at = turn * HALVES + half
        return sending(
            "dp", owners, dp_send.at[at], dp_recv.at[at], dp_ssem.at[at], dp_rsem.at[at]
        )

    def send_cells(turn, half, coarse):
        wide = jnp.concatenate(
            [coarse[:, j * group : (j + 1) * group].T.astype(bf16) for j in range(quads)], axis=1
        )
        wide = dot(wide, regroup[...])
        for block in range(blocks):
            at = block * 2 * near
            pieces = [wide[at : at + 2 * near, x * lanes : (x + 1) * lanes] for x in range(slab)]
            space_send[turn * HALVES + half, block] = jnp.concatenate(pieces, axis=0).astype(bf16)
        return send_space(turn, half)

    def cells_to_modes(turn, dp_turn, arriving):
        copies = []
        for half in range(HALVES):
            wait_arrivals(arriving[half])
            cells[half] = space_recv[turn * HALVES + half].astype(f32).reshape(cells.shape[1:])
            wide = jnp.concatenate(
                [cells[half, pl.ds(t, blocks * 2 * slab, stride=near), :] for t in range(near)],
                axis=1,
            ).astype(bf16)
            spectrum = dot(line[...], wide).astype(bf16)
            dp_send[dp_turn * HALVES + half] = spectrum.reshape(owners, 2 * kept, near * lanes)
            copies.append(send_dp(dp_turn, half))
        return copies

    def modes_to_cells(dp_turn, turn, arriving):
        copies = []
        for half in range(HALVES):
            wait_arrivals(arriving[half])
            wide = dp_recv[dp_turn * HALVES + half].reshape(rows, near * lanes)
            back = lax.dot_general(line[...], wide, TN, preferred_element_type=f32)
            for t in range(near):
                cells[half, pl.ds(t, blocks * 2 * slab, stride=near), :] = back[
                    :, t * lanes : (t + 1) * lanes
                ]
            space_send[turn * HALVES + half] = (
                cells[half].astype(bf16).reshape(space_send.shape[1:])
            )
            copies.append(send_space(turn, half))
        return copies

    def stack_half(dp_turn, half):
        for t in range(near):
            stack[t * rows : (t + 1) * rows] = dp_recv[
                dp_turn * HALVES + half, :, :, t * lanes : (t + 1) * lanes
            ].reshape(rows, lanes)

    def unstack_half(dp_turn, half, values):
        for t in range(near):
            dp_send[dp_turn * HALVES + half, :, :, t * lanes : (t + 1) * lanes] = (
                values[t * rows : (t + 1) * rows].astype(bf16).reshape(owners, 2 * kept, lanes)
            )
        return send_dp(dp_turn, half)

    def weight_tiles(m, s):
        lo = s * 128
        return (
            weights[m, :, lo : lo + 128].astype(f32),
            weights[m, :, square + lo : square + lo + 128].astype(f32),
        )

    to_lines(feats, rows_in)

    def analyse(half, source):
        at = slice(half * part_columns, (half + 1) * part_columns)
        coarse_acc[...] = jnp.zeros_like(coarse_acc)
        for step in range(chunks):
            if half == 0 and source is rows_in:
                analysis_loads[step].wait()
            rows_at = slice(step * chunk, (step + 1) * chunk)
            coarse_acc[...] += dot(source[:, rows_at], analysis[rows_at, at])
        return coarse_acc[...]

    coarse = analyse(0, rows_in)
    pl.semaphore_wait(barrier, blocks + owners - 2)
    load_tables[0].wait()
    copies = [send_cells(0, 0, coarse)]
    for half in range(1, HALVES):
        copies.append(send_cells(0, half, analyse(half, rows_in)))

    same_cell = lax.rem(lax.broadcasted_iota(jnp.int32, mix_fwd.shape, 0), slab) == lax.rem(
        lax.broadcasted_iota(jnp.int32, mix_fwd.shape, 1), slab
    )
    spread_out = dot_nt(dot_nt(repeat[...], pointwise[...]).astype(bf16), repeat[...])
    mix_fwd[...] = jnp.where(same_cell, spread_out, 0.0).astype(bf16)
    spread_out = dot_nt(dot(repeat[...], pointwise[...]).astype(bf16), repeat[...])
    mix_back[...] = jnp.where(same_cell, spread_out, 0.0).astype(bf16)
    bias[...] = jnp.sum(
        repeat[...].astype(f32) * biases[...].astype(f32), axis=1, keepdims=True
    )
    load_cot.wait()
    to_lines(cot, upstream)

    copies = cells_to_modes(0, 0, copies)

    def prepare(step, _):
        at = columns(step)
        linear[:, at] = dot(mix_fwd[...], rows_in[:, at]) + bias[...]
        return 0

    lax.fori_loop(0, chunks, prepare, 0)
    load_weights.wait()
    for copy in load_tables[1:]:
        copy.wait()

    back_copies = []
    for half in range(HALVES):
        wait_arrivals(copies[half])
        stack_half(0, half)

        def mix(j, _, half=half):
            spec_wide[half, j] = dot(stack[...], spread[j])
            for t in range(near):
                m = (half * near + t) * quads + j
                base = t * rows
                total = [None] * (2 * owners)
                for s in range(square // 128):
                    lo = s * 128
                    w_re, w_im = weight_tiles(m, s)
                    for n in range(owners):
                        at = base + 2 * n * kept
                        re = spec_wide[half, j, at : at + kept, lo : lo + 128]
                        im = spec_wide[half, j, at + kept : at + 2 * kept, lo : lo + 128]
                        out_re = re * w_re - im * w_im
                        out_im = re * w_im + im * w_re
                        total[2 * n] = out_re if s == 0 else total[2 * n] + out_re
                        total[2 * n + 1] = out_im if s == 0 else total[2 * n + 1] + out_im
                parts[j, base : base + rows, :] = jnp.concatenate(total, axis=0).astype(bf16)
            return 0

        lax.fori_loop(0, quads, mix, 0)
        mixed = dot(jnp.concatenate([parts[j] for j in range(quads)], axis=1), tile[...])
        back_copies.append(unstack_half(1, half, mixed))
    copies = modes_to_cells(1, 1, back_copies)
    load_synthesis.wait()
    for half in range(HALVES):
        wait_arrivals(copies[half])
        collect_volume(
            slab, half, space_recv.at[HALVES + half], regroup, volume, doubling
        )

    def activate(step, _):
        at = columns(step)
        pre_act = dot(volume[...], synthesis[:, at]) + linear[:, at]
        delta[:, at] = (upstream[:, at] * gelu_slope(pre_act)).astype(bf16)
        return 0

    lax.fori_loop(0, chunks, activate, 0)
    copies = []
    for half in range(HALVES):
        at = slice(half * part_columns, (half + 1) * part_columns)
        copies.append(send_cells(2, half, analyse(half, delta) * doubling[:, at]))
    store_delta = pltpu.make_async_copy(delta, out_delta, load_sem.at[4])
    store_delta.start()
    copies = cells_to_modes(2, 2, copies)

    back_copies = []
    for half in range(HALVES):
        wait_arrivals(copies[half])
        stack_half(2, half)
        wide = dot(stack[...], untile[...])
        for j in range(quads):
            adj_wide[half, j] = wide[:, j * lanes : (j + 1) * lanes]
        pulled[...] = jnp.zeros_like(pulled)

        def pull(j, _, half=half):
            for t in range(near):
                m = (half * near + t) * quads + j
                base = t * rows
                adjs = [
                    adj_wide[half, j, base + r * kept : base + (r + 1) * kept]
                    for r in range(2 * owners)
                ]
                for s in range(square // 128):
                    w_re, w_im = weight_tiles(m, s)
                    terms = []
                    for n in range(owners):
                        re, im = adjs[2 * n], adjs[2 * n + 1]
                        terms += [re * w_re + im * w_im, im * w_re - re * w_im]
                    products[base : base + rows, s * 128 : (s + 1) * 128] = jnp.concatenate(
                        terms, axis=0
                    ).astype(bf16)
            pulled[...] += dot(products[...], gather[j])
            return 0

        lax.fori_loop(0, quads, pull, 0)
        back_copies.append(unstack_half(3, half, pulled[...]))

    for half in range(HALVES):

        def weight_terms(j, _, half=half):
            for t in range(near):
                m = (half * near + t) * quads + j
                base = t * rows
                adjs = [
                    adj_wide[half, j, base + r * kept : base + (r + 1) * kept]
                    for r in range(2 * owners)
                ]
                for s in range(square // 128):
                    lo = s * 128
                    grad_re, grad_im = None, None
                    for n in range(owners):
                        at = base + 2 * n * kept
                        re = spec_wide[half, j, at : at + kept, lo : lo + 128]
                        im = spec_wide[half, j, at + kept : at + 2 * kept, lo : lo + 128]
                        a_re, a_im = adjs[2 * n], adjs[2 * n + 1]
                        term_re = re * a_re + im * a_im
                        term_im = re * a_im - im * a_re
                        grad_re = term_re if n == 0 else grad_re + term_re
                        grad_im = term_im if n == 0 else grad_im + term_im
                    grads[m, :, lo : lo + 128] = grad_re
                    grads[m, :, square + lo : square + lo + 128] = grad_im
            return 0

        lax.fori_loop(0, quads, weight_terms, 0)
    store_grads = pltpu.make_async_copy(grads, out_grads, load_sem.at[3])
    store_grads.start()
    copies = modes_to_cells(3, 3, back_copies)
    for half in range(HALVES):
        wait_arrivals(copies[half])
        out_cells[half] = space_recv[3 * HALVES + half]
    store_delta.wait()
    store_grads.wait()
    for copy in sent:
        copy.wait_send()


def collect_volume(slab, half, arrived, regroup, volume, doubling):
    blocks, lanes = arrived.shape[0], arrived.shape[2]
    tile_rows = arrived.shape[1] // slab
    group = blocks * tile_rows
    pieces = []
    for block in range(blocks):
        held = arrived[block].astype(f32)
        pieces.append(
            jnp.concatenate(
                [held[x * tile_rows : (x + 1) * tile_rows] for x in range(slab)], axis=1
            )
        )
    wide = dot_nt(jnp.concatenate(pieces, axis=0).astype(bf16), regroup[...])
    quads = wide.shape[1] // lanes
    for j in range(quads):
        at = slice((half * quads + j) * group, (half * quads + j + 1) * group)
        part = wide[:, j * lanes : (j + 1) * lanes].T
        if doubling is not None:
            part = part * doubling[:, at]
        volume[:, at] = part.astype(bf16)


def result_kernel(
    slab, arrived, mix_back, regroup, delta_hbm, grads_hbm, synthesis_hbm,
    out_input, out_spectral,
    delta, grads, synthesis, volume, lined, natural, sems, synthesis_sem, out_sem,
):
    cell_rows, cells_count = delta.shape
    chunks = synthesis_sem.shape[0]
    chunk = cells_count // chunks
    span_y, width = natural.shape[1:]
    load_delta = pltpu.make_async_copy(delta_hbm, delta, sems.at[0])
    load_delta.start()
    loads = [
        pltpu.make_async_copy(
            synthesis_hbm.at[:, pl.ds(step * chunk, chunk)],
            synthesis.at[:, pl.ds(step * chunk, chunk)],
            synthesis_sem.at[step],
        )
        for step in range(chunks)
    ]
    for copy in loads:
        copy.start()
    load_grads = pltpu.make_async_copy(grads_hbm, grads, sems.at[1])
    load_grads.start()
    for half in range(HALVES):
        collect_volume(slab, half, arrived.at[half], regroup, volume, None)
    load_delta.wait()
    parts = out_sem.shape[0]
    part_y = span_y // parts
    stores = []
    for part in range(parts):
        for step in range(part * chunks // parts, (part + 1) * chunks // parts):
            loads[step].wait()
            at = slice(step * chunk, (step + 1) * chunk)
            lined[:, at] = dot(volume[...], synthesis[:, at]) + dot(mix_back[...], delta[:, at])

        def swap(step, _, part=part):
            at = pl.ds(pl.multiple_of(step * 8, 8), 8)
            stacked = jnp.stack(
                [
                    lined[at, y * width : (y + 1) * width]
                    for y in range(part * part_y, (part + 1) * part_y)
                ],
                axis=0,
            )
            natural[at, part * part_y : (part + 1) * part_y, :] = jnp.swapaxes(
                stacked, 0, 1
            ).astype(bf16)
            return 0

        lax.fori_loop(0, cell_rows // 8, swap, 0)
        copy = pltpu.make_async_copy(
            natural.at[:, pl.ds(part * part_y, part_y), :],
            out_input.at[:, pl.ds(part * part_y, part_y), :],
            out_sem.at[part],
        )
        copy.start()
        stores.append(copy)
        if part == 0:
            load_grads.wait()
            store_grads = pltpu.make_async_copy(grads, out_spectral, sems.at[2])
            store_grads.start()
            stores.append(store_grads)
    wait_all(stores)


def fits(features, spectral, owners):
    samples, channels, slab, span_y, span_z = features.shape
    modes, kept = spectral.shape[:2]
    return (
        samples == 1 and kept == 8 and channels == 32 and slab == 4 and modes == 32
        and span_z == 128 and span_y % 16 == 0 and (2 * kept * owners) % 16 == 0
    )


def body(features, cotangent, spectral, pointwise, biases):
    blocks, owners = lax.axis_size("space"), lax.axis_size("dp")
    if not fits(features, spectral, owners):
        return plain_body(features, cotangent, spectral, pointwise, biases)
    _, channels, slab, span_y, span_z = features.shape
    modes, kept = spectral.shape[:2]
    tiles = 8
    quads = modes // tiles
    lanes = quads * channels
    square = channels * channels
    cell_rows, cells_count = channels * slab, span_y * span_z
    natural_shape = (cell_rows, span_y, span_z)
    plane, doubling = np_plane_rows(span_y, span_z, blocks, tiles, quads)
    line = np_line(slab * blocks, blocks, owners)
    plane_rows = plane.shape[0]
    chunks = 8
    rows = 2 * kept * owners
    half_rows = rows * tiles // HALVES
    sizes = (blocks, owners, channels, slab, span_y, tiles, quads, kept)
    vmem = pl.BlockSpec(memory_space=pltpu.VMEM)
    hbm = pl.BlockSpec(memory_space=pl.ANY)
    space_shape = (4 * HALVES, blocks, 2 * slab * tiles // HALVES, lanes)
    dp_shape = (4 * HALVES, owners, 2 * kept, tiles // HALVES * lanes)
    regroup, spread, gather, tile, untile, repeat = np_selectors(channels, slab, quads)
    arrived, delta, grads, mix_back = pl.pallas_call(
        functools.partial(layer_kernel, sizes),
        out_shape=(
            jax.ShapeDtypeStruct((HALVES,) + space_shape[1:], bf16),
            jax.ShapeDtypeStruct((cell_rows, cells_count), bf16),
            jax.ShapeDtypeStruct(spectral.shape, f32),
            jax.ShapeDtypeStruct((cell_rows, cell_rows), bf16),
        ),
        in_specs=[vmem, hbm, hbm, vmem, vmem] + [hbm] * 7 + [vmem] * 3,
        out_specs=(vmem, hbm, hbm, vmem),
        scratch_shapes=[
            pltpu.VMEM(natural_shape, bf16),
            pltpu.VMEM(spectral.shape, bf16),
            pltpu.VMEM((cells_count, plane_rows), bf16),
            pltpu.VMEM((plane_rows, cells_count), bf16),
            pltpu.VMEM(regroup.shape, bf16),
            pltpu.VMEM(spread.shape, bf16),
            pltpu.VMEM(gather.shape, bf16),
            pltpu.VMEM(tile.shape, bf16),
            pltpu.VMEM(untile.shape, bf16),
            pltpu.VMEM(spectral.shape, f32),
            pltpu.VMEM((cell_rows, cells_count), bf16),
            pltpu.VMEM((cell_rows, cells_count), f32),
            pltpu.VMEM((cell_rows, cells_count), f32),
            pltpu.VMEM((cell_rows, cells_count), bf16),
            pltpu.VMEM((cell_rows, plane_rows // HALVES), f32),
            pltpu.VMEM((cell_rows, plane_rows), bf16),
            pltpu.VMEM((cell_rows, cell_rows), bf16),
            pltpu.VMEM((cell_rows, 1), f32),
            pltpu.VMEM((half_rows, lanes), bf16),
            pltpu.VMEM((quads, half_rows, lanes), bf16),
            pltpu.VMEM((HALVES, quads, half_rows, square), f32),
            pltpu.VMEM((HALVES, quads, half_rows, lanes), f32),
            pltpu.VMEM((half_rows, square), bf16),
            pltpu.VMEM((half_rows, lanes), f32),
            pltpu.VMEM((HALVES, blocks * 2 * slab * tiles // HALVES, lanes), f32),
            pltpu.VMEM(space_shape, bf16),
            pltpu.VMEM(space_shape, bf16),
            pltpu.VMEM(dp_shape, bf16),
            pltpu.VMEM(dp_shape, bf16),
            pltpu.SemaphoreType.DMA((10,)),
            pltpu.SemaphoreType.DMA((chunks,)),
            pltpu.SemaphoreType.DMA((4 * HALVES, blocks)),
            pltpu.SemaphoreType.DMA((4 * HALVES, blocks)),
            pltpu.SemaphoreType.DMA((4 * HALVES, owners)),
            pltpu.SemaphoreType.DMA((4 * HALVES, owners)),
        ],
        compiler_params=pltpu.CompilerParams(
            collective_id=0, has_side_effects=True, vmem_limit_bytes=56 * 1024 * 1024
        ),
    )(
        features.reshape(natural_shape),
        cotangent.reshape(natural_shape),
        spectral, pointwise, biases[None, :],
        np.ascontiguousarray(plane.T), plane,
        regroup, spread, gather, tile, untile, repeat, doubling.T, line,
    )
    grad_input, grad_spectral = pl.pallas_call(
        functools.partial(result_kernel, slab),
        out_shape=(
            jax.ShapeDtypeStruct(natural_shape, bf16),
            jax.ShapeDtypeStruct(spectral.shape, f32),
        ),
        in_specs=[vmem, vmem, vmem, hbm, hbm, hbm],
        out_specs=(hbm, hbm),
        scratch_shapes=[
            pltpu.VMEM((cell_rows, cells_count), bf16),
            pltpu.VMEM(spectral.shape, f32),
            pltpu.VMEM((plane_rows, cells_count), bf16),
            pltpu.VMEM((cell_rows, plane_rows), bf16),
            pltpu.VMEM((cell_rows, cells_count), f32),
            pltpu.VMEM(natural_shape, bf16),
            pltpu.SemaphoreType.DMA((3,)),
            pltpu.SemaphoreType.DMA((chunks,)),
            pltpu.SemaphoreType.DMA((span_y // 16,)),
        ],
        compiler_params=pltpu.CompilerParams(vmem_limit_bytes=20 * 1024 * 1024),
    )(arrived, mix_back, regroup, delta, grads, plane)
    return grad_input.reshape(features.shape), grad_spectral


def solution(mesh):
    placed = (
        P("dp", None, "space", None, None),
        P("dp", None, "space", None, None),
        P("space", "dp", None),
        P(),
        P(),
    )
    return jax.shard_map(
        body,
        mesh=mesh,
        in_specs=placed,
        out_specs=(P("dp", None, "space", None, None), P("space", "dp", None)),
        check_vma=False,
    )
```
